256 devices in a mesh: dp: 8 (over y, core), shard: 32 (over x, z).
Axes of the slice: x: 4, y: 4, z: 8, core: 2. Of those that a mesh axis runs over, the one named last changes fastest.
Arguments:
- grads: bfloat16 [8, 36, 1024, 1024], P('dp', None, 'shard'), may hold values from -0.59765625 to 0.59765625
- vec_grads: bfloat16 [8, 32, 1024], P('dp', 'shard'), may hold values from -0.59765625 to 0.59765625
- factor_left: float32 [96, 1024, 1024], P('shard', 'dp'), may hold values from -6 to 6
- factor_right: float32 [96, 1024, 1024], P('shard', None, 'dp'), may hold values from -6 to 6
- root_left: bfloat16 [96, 1024, 1024], P('shard', None, 'dp'), may hold values from -0.1875 to 0.1875
- root_right: bfloat16 [96, 1024, 1024], P('shard', None, 'dp'), may hold values from -0.1875 to 0.1875
- vec_param: float32 [32, 1024], P('shard', 'dp'), may hold values from -10 to 10
- vec_first: float32 [32, 1024], P('shard', 'dp'), may hold values from -0.6 to 0.6
- vec_second: float32 [32, 1024], P('shard', 'dp'), may hold values from 0.001 to 0.1
- bucket_block: int32 [36], replicated, may hold values from 0 to 35, each once
- block_slot: int32 [36], replicated, may hold values from 0 to 95, as said below
- decay_mask: int32 [32, 1024], P('shard', 'dp'), may hold values 0 or 1
Outputs:
- block_update: bfloat16 [36, 1024, 1024], P(None, 'shard')
- new_left: float32 [96, 1024, 1024], P('shard', 'dp')
- new_right: float32 [96, 1024, 1024], P('shard', None, 'dp')
- vec_update: bfloat16 [32, 1024], P('shard')
- new_first: float32 [32, 1024], P('shard', 'dp')
- new_second: float32 [32, 1024], P('shard', 'dp')
The draws below stay inside these ranges and needn't reach their ends.
Inputs may be any that keep to these rules, and one draw needn't show every extreme that they name: `bucket_block`: a permutation of the block numbers. `block_slot`: distinct values; a value's owner is value // 3 and its place there value % 3; no owner holds more than 3 blocks and some owner holds exactly 3.
All inputs are finite; a program needn't handle non-finite values. No bound on the sum of `decay_mask` on one device may be relied on, other than what follows from the above.
Results may differ from the reference program's by a relative error of at most 0.022.
Values may be sent and summed in bfloat16 or wider, within the bound.
No kernel may reach another device: no remote copies, remote signals or barrier semaphores. Data moves between devices by JAX's collectives and lax.ppermute only.
A program may use at most 128 MiB of HBM per device.

```python
import math
import jax
import jax.numpy as jnp
from jax import lax

BLOCK = 1024
SLOTS = 3
VCOLS = 1024
VROWS = 32
NBLK = 36
SLOT_ALL = 96
N_DP = 8
N_SHARD = 32


def draw_block_slot(key, part):
    key = jax.random.fold_in(key, 11)
    key_owner, key_rank, key_order = jax.random.split(key, 3)
    slot_total = SLOTS * N_SHARD
    slot_ids = jnp.arange(slot_total, dtype=jnp.int32)
    chosen_owner = jax.random.randint(key_owner, (), 0, N_SHARD, dtype=jnp.int32)
    ranking = jax.random.permutation(key_rank, slot_total).astype(jnp.int32)
    favoured = (slot_ids // SLOTS == chosen_owner) | (slot_ids == 0) | (slot_ids == slot_total - 1)
    scores = ranking + jnp.where(favoured, -slot_total, 0).astype(jnp.int32)
    ordering = jnp.argsort(scores, stable=True).astype(jnp.int32)
    picked = ordering[:NBLK]
    return jax.random.permutation(key_order, picked).astype(jnp.int32)


def touch_ends(entries, own_key, least, top_value):
    dims = entries.shape
    place = [jax.random.randint(jax.random.fold_in(own_key, axis), (), 0, dims[axis]) for axis in range(len(dims))]
    entries = entries.at[tuple(place)].set(least)
    longest = dims.index(max(dims))
    place[longest] = (place[longest] + 1) % dims[longest]
    return entries.at[tuple(place)].set(top_value)


def raised(result, stream_key, source, target, shards_of, factor):
    owner, partner = [(jnp.arange(result.shape[axis_at]) // (result.shape[axis_at] // shards_of)).reshape([-1 if axis == axis_at else 1 for axis in range(result.ndim)]) for axis_at in (source, target)]
    chosen = jax.random.permutation(stream_key, shards_of)[partner]
    strong = (owner == chosen) | (owner == (partner + shards_of // 2) % shards_of)
    return jnp.where(strong, factor * result, result)


def block_levels(rng, shape, pieces, least, top_value):
    def one(dim, parts):
        draws = jax.random.uniform(jax.random.fold_in(jax.random.fold_in(rng, 6), dim), (parts,), jnp.float32, least / len(pieces), top_value / len(pieces))
        return jnp.repeat(jnp.exp(draws), shape[dim] // parts).reshape((-1,) + (1,) * (len(shape) - dim - 1))

    factor_of = one(*pieces[0])
    for cut in pieces[1:]:
        factor_of = factor_of * one(*cut)
    return factor_of


def noise(stream_key, shape, spread, limit, shards=(), kind=jnp.bfloat16):
    factor_of = block_levels(stream_key, shape, shards, -0.22, 0.18) if shards else 1.0
    result = jax.random.normal(stream_key, shape, jnp.float32) * spread * factor_of
    return jnp.minimum(jnp.maximum(result, -limit), limit).astype(kind)


def noise_with(rng, dims, width, reach, cuts, heavy, held_as=jnp.bfloat16):
    result = width * jax.random.normal(rng, dims, jnp.float32)
    if cuts:
        result = result * block_levels(rng, dims, cuts, -0.22, 0.18)
    return jnp.clip(raised(result, jax.random.fold_in(rng, 3), *heavy), -reach, reach).astype(held_as)


def setup_inputs(seed: int = 0) -> dict:
    key_of = jax.random.split(jax.random.key(seed), 13)
    return {
        "grads": noise_with(key_of[0], (N_DP, NBLK, BLOCK, BLOCK), 0.1, 0.59765625, ((0, 8), (2, 32)), (0, 3, 8, 2.0)),
        "vec_grads": noise(key_of[1], (N_DP, VROWS, VCOLS), 0.1, 0.59765625, ((0, 8), (1, 32))),
        "factor_left": noise(key_of[2], (SLOT_ALL, BLOCK, BLOCK), 1.0, 6.0, ((0, 32), (1, 8)), jnp.float32),
        "factor_right": noise(key_of[3], (SLOT_ALL, BLOCK, BLOCK), 1.0, 6.0, ((0, 32), (2, 8)), jnp.float32),
        "root_left": noise(key_of[4], (SLOT_ALL, BLOCK, BLOCK), BLOCK ** -0.5, 0.1875, ((0, 32), (2, 8))),
        "root_right": noise(key_of[5], (SLOT_ALL, BLOCK, BLOCK), BLOCK ** -0.5, 0.1875, ((0, 32), (2, 8))),
        "vec_param": noise(key_of[6], (VROWS, VCOLS), 2.0, 10.0, ((0, 32), (1, 8)), jnp.float32),
        "vec_first": noise(key_of[7], (VROWS, VCOLS), 0.1, 0.6, ((0, 32), (1, 8)), jnp.float32),
        "vec_second": jnp.clip(jnp.exp(math.log(0.1) - 4.6051702 * jax.random.uniform(key_of[8], (VROWS, VCOLS), jnp.float32) ** block_levels(key_of[8], (VROWS, VCOLS), ((0, 32), (1, 8)), -0.2, 0.2)), 0.001, 0.1),
        "bucket_block": jax.random.permutation(key_of[9], NBLK).astype(jnp.int32),
        "block_slot": draw_block_slot(jax.random.fold_in(key_of[12], 71), 0),
        "decay_mask": touch_ends((jax.random.randint(key_of[11], (VROWS, VCOLS), 0, 2) < 1).astype(jnp.int32), jax.random.fold_in(key_of[11], 1), 0, 1),
    }


BETA_STAT = 0.95
ADAM_ONE = 0.9
ADAM_TWO = 0.95
ADAM_EPS = 1e-08
DECAY = 0.1

def reference(grads, vec_grads, factor_left, factor_right, root_left, root_right, vec_param, vec_first, vec_second, bucket_block, block_slot, decay_mask):
    accum = jnp.zeros(grads.shape[1:], jnp.float32)
    for replica in range(grads.shape[0]):
        accum = accum + grads[replica].astype(jnp.float32)
    summed = accum.astype(jnp.bfloat16)
    slot_of = jnp.take(block_slot, bucket_block).astype(jnp.int32)

    def per_block(item):
        grad_block, slot_id = item
        gram_rows = jnp.dot(grad_block, grad_block.T, preferred_element_type=jnp.float32)
        gram_cols = jnp.dot(grad_block.T, grad_block, preferred_element_type=jnp.float32)
        right_applied = jnp.dot(grad_block, root_right[slot_id], preferred_element_type=jnp.float32).astype(jnp.bfloat16)
        update = jnp.dot(root_left[slot_id], right_applied, preferred_element_type=jnp.float32).astype(jnp.bfloat16)
        return (gram_rows, gram_cols, update)
    gram_rows, gram_cols, block_update = lax.map(per_block, (summed, slot_of))
    new_left = (BETA_STAT * factor_left).at[slot_of].add((1.0 - BETA_STAT) * gram_rows)
    new_right = (BETA_STAT * factor_right).at[slot_of].add((1.0 - BETA_STAT) * gram_cols)
    vec_sum = jnp.zeros(vec_grads.shape[1:], jnp.float32)
    for replica in range(vec_grads.shape[0]):
        vec_sum = vec_sum + vec_grads[replica].astype(jnp.float32)
    new_first = ADAM_ONE * vec_first + (1.0 - ADAM_ONE) * vec_sum
    new_second = ADAM_TWO * vec_second + (1.0 - ADAM_TWO) * vec_sum * vec_sum
    vec_update = (new_first / (jnp.sqrt(new_second) + ADAM_EPS) + DECAY * decay_mask.astype(jnp.float32) * vec_param).astype(jnp.bfloat16)
    return (block_update, new_left, new_right, vec_update, new_first, new_second)
```

```python
import jax
import jax.numpy as jnp
from jax import lax
from jax.experimental import pallas as pl
from jax.experimental.pallas import tpu as pltpu
from jax.sharding import Mesh
from jax.sharding import PartitionSpec as P

BETA_STAT = 0.95
ADAM_ONE = 0.9
ADAM_TWO = 0.95
ADAM_EPS = 1e-08
DECAY = 0.1

RING = 4
CORES = 2
OWNERS = 32
SLOTS = 3
NBLK = 36
PER = NBLK // RING
BLOCK = 1024
ROWS = BLOCK // OWNERS
TILE = 128
HALF = BLOCK // CORES
BODY = PER * ROWS
PIECE = BODY + 16
FULL = NBLK * ROWS
BF16 = jnp.bfloat16
F32 = jnp.float32
T_OWNER = NBLK
T_SEL = 2 * NBLK
T_REL = T_SEL + RING
VMEM_LIMIT = 40 * 1024 * 1024


def whole():
    return pl.BlockSpec(memory_space=pltpu.VMEM)


def call(body, grid, in_specs, out_specs, out_shape, scratch=(), flops=0, moved=0):
    return pl.pallas_call(
        body,
        grid_spec=pltpu.PrefetchScalarGridSpec(
            num_scalar_prefetch=2,
            grid=grid,
            in_specs=in_specs,
            out_specs=out_specs,
            scratch_shapes=list(scratch),
        ),
        out_shape=out_shape,
        compiler_params=pltpu.CompilerParams(vmem_limit_bytes=VMEM_LIMIT),
        cost_estimate=pl.CostEstimate(flops=flops, bytes_accessed=moved, transcendentals=0),
    )


def tile_at(index):
    return pl.ds(pl.multiple_of(index * TILE, TILE), TILE)


def rows_at(index, size=ROWS):
    return pl.ds(pl.multiple_of(index * size, size), size)


def dot(a, b):
    return jnp.dot(a, b, preferred_element_type=F32)


def pick_body(pos, tab, grad, vec, out):
    out[0:FULL, :] = grad[...]
    out[FULL : FULL + 16, :] = vec[...]


def pick(pos, tab, grad, vec):
    other = lambda j, pos, tab: (0, 2 * j + 1 - pos[1])
    return call(
        pick_body,
        (RING,),
        [pl.BlockSpec((FULL, TILE), other), pl.BlockSpec((16, TILE), other)],
        pl.BlockSpec((FULL + 16, TILE), lambda j, pos, tab: (0, j)),
        jax.ShapeDtypeStruct((FULL + 16, HALF), BF16),
        moved=4 * FULL * HALF,
    )(pos, tab, grad, vec)


def pair_body(pos, tab, grad, vec, got, *outs):
    strip = (vec[...].astype(F32) + got[FULL : FULL + 16, :].astype(F32)).astype(BF16)
    for k in range(RING):
        plane = lax.rem(pos[0] + k, RING)
        for i in range(PER):
            at = rows_at(tab[RING * i + plane])
            both = grad[at, :].astype(F32) + got[at, :].astype(F32)
            outs[k][ROWS * i : ROWS * (i + 1), :] = both.astype(BF16)
        outs[k][BODY:PIECE, :] = strip


def pair(pos, tab, grad, vec, got):
    mine = lambda j, pos, tab: (0, 2 * j + pos[1])
    here = lambda j, pos, tab: (0, j)
    return call(
        pair_body,
        (RING,),
        [
            pl.BlockSpec((FULL, TILE), mine),
            pl.BlockSpec((16, TILE), mine),
            pl.BlockSpec((FULL + 16, TILE), here),
        ],
        [pl.BlockSpec((PIECE, TILE), here)] * RING,
        [jax.ShapeDtypeStruct((PIECE, HALF), BF16)] * RING,
        moved=6 * FULL * HALF,
    )(pos, tab, grad, vec, got)


def total_body(pos, tab, a, b, c, d, param, first, second, mask, send, new_first, new_second, step):
    send[...] = jnp.zeros(send.shape, BF16)
    for i in range(PER):
        at = slice(ROWS * i, ROWS * (i + 1))
        total = (a[at, :].astype(F32) + b[at, :].astype(F32)) + (
            c[at, :].astype(F32) + d[at, :].astype(F32)
        )
        send[rows_at(tab[T_OWNER + RING * i + pos[0]]), :] = total.astype(BF16)
    lanes = tile_at(pos[0])
    strips = [ref[BODY:PIECE, lanes].astype(F32) for ref in (a, b, c, d)]
    vec_sum = ((strips[0] + strips[1]) + (strips[2] + strips[3]))[0:1]
    one = ADAM_ONE * first[...] + (1.0 - ADAM_ONE) * vec_sum
    two = ADAM_TWO * second[...] + (1.0 - ADAM_TWO) * vec_sum * vec_sum
    new_first[...] = one
    new_second[...] = two
    update = one / (jnp.sqrt(two) + ADAM_EPS) + DECAY * mask[...].astype(F32) * param[...]
    step[...] = jnp.broadcast_to(update, (16, TILE)).astype(BF16)


def total(pos, tab, parts, param, first, second, mask):
    return call(
        total_body,
        (),
        [whole()] * 8,
        [whole()] * 4,
        [
            jax.ShapeDtypeStruct((BLOCK, HALF), BF16),
            jax.ShapeDtypeStruct((1, TILE), F32),
            jax.ShapeDtypeStruct((1, TILE), F32),
            jax.ShapeDtypeStruct((16, TILE), BF16),
        ],
        moved=8 * PIECE * HALF + 2 * BLOCK * HALF,
    )(pos, tab, *parts, param, first, second, mask)


def roots_body(pos, tab, left, left_other, right, *outs):
    for k in range(RING):
        slot = tab[T_SEL + k]
        outs[k][0:BLOCK, :] = left[slot]
        outs[k][BLOCK : 2 * BLOCK, :] = left_other[slot]
        outs[k][2 * BLOCK : 3 * BLOCK, :] = right[slot]


def roots(pos, tab, left, left_other, right):
    return call(
        roots_body,
        (),
        [whole()] * 3,
        [whole()] * RING,
        [jax.ShapeDtypeStruct((3 * BLOCK, TILE), BF16)] * RING,
        moved=2 * (3 + RING) * 3 * BLOCK * TILE,
    )(pos, tab, left, left_other, right)


def update_body(pos, tab, mine, other, r0, r1, r2, r3, out, grad, left, right, applied):
    core = pos[1]
    for j in range(RING):
        lanes = slice(TILE * j, TILE * (j + 1))
        grad[:, tile_at(2 * j + core)] = mine[:, lanes]
        grad[:, tile_at(2 * j + 1 - core)] = other[:, lanes]
    for k, ref in enumerate((r0, r1, r2, r3)):
        plane = lax.rem(pos[0] + RING - k, RING)
        left[:, tile_at(2 * plane + core)] = ref[0:BLOCK, :]
        left[:, tile_at(2 * plane + 1 - core)] = ref[BLOCK : 2 * BLOCK, :]
        right[:, tile_at(plane)] = ref[2 * BLOCK : 3 * BLOCK, :]
    step = 256

    @pl.loop(0, BLOCK // step)
    def _(i):
        at = rows_at(i, step)
        applied[at, :] = dot(grad[at, :], right[...]).astype(BF16)

    @pl.loop(0, BLOCK // step)
    def _(i):
        at = rows_at(i, step)
        out[at, :] = dot(left[at, :], applied[...]).astype(BF16)


def update(pos, tab, mine, other, parts):
    return call(
        update_body,
        (),
        [whole()] * 6,
        whole(),
        jax.ShapeDtypeStruct((BLOCK, HALF), BF16),
        scratch=[
            pltpu.VMEM((BLOCK, BLOCK), BF16),
            pltpu.VMEM((BLOCK, BLOCK), BF16),
            pltpu.VMEM((BLOCK, HALF), BF16),
            pltpu.VMEM((BLOCK, HALF), BF16),
        ],
        flops=4 * BLOCK * BLOCK * HALF,
        moved=16 * BLOCK * HALF,
    )(pos, tab, mine, other, *parts)


def gram_body(pos, tab, mine, other, o0, o1, o2, o3, grad, turned):
    core = pos[1]
    for j in range(RING):
        lanes = slice(TILE * j, TILE * (j + 1))
        grad[:, tile_at(2 * j + core)] = mine[:, lanes]
        grad[:, tile_at(2 * j + 1 - core)] = other[:, lanes]

    @pl.loop(0, BLOCK // TILE)
    def _(t):
        turned[:, tile_at(t)] = grad[rows_at(t, TILE), :].T

    for k, ref in enumerate((o0, o1, o2, o3)):
        plane = lax.rem(pos[0] + k, RING)
        rows = dot(grad[rows_at(2 * plane + core, TILE), :], turned[...])
        for t in range(BLOCK // TILE):
            ref[TILE * t : TILE * (t + 1), :] = rows[:, TILE * t : TILE * (t + 1)].astype(BF16)

    for k, ref in enumerate((o0, o1, o2, o3)):
        plane = lax.rem(pos[0] + k, RING)
        ref[BLOCK : 2 * BLOCK, :] = dot(turned[...], mine[:, tile_at(plane)]).astype(BF16)


def gram(pos, tab, mine, other):
    return call(
        gram_body,
        (),
        [whole()] * 2,
        [whole()] * RING,
        [jax.ShapeDtypeStruct((2 * BLOCK, TILE), BF16)] * RING,
        scratch=[pltpu.VMEM((BLOCK, BLOCK), BF16), pltpu.VMEM((BLOCK, BLOCK), BF16)],
        flops=4 * BLOCK * BLOCK * HALF,
        moved=8 * BLOCK * HALF,
    )(pos, tab, mine, other)


def stats_body(pos, tab, left, right, g0, g1, g2, g3, new_left, new_right):
    source = tab[T_REL + pl.program_id(0)]

    @pl.when(source < 0)
    def _():
        new_left[...] = BETA_STAT * left[...]
        new_right[...] = BETA_STAT * right[...]

    for k, ref in enumerate((g0, g1, g2, g3)):

        @pl.when(source == k)
        def _(ref=ref):
            for t in range(BLOCK // TILE):
                at = slice(TILE * t, TILE * (t + 1))
                add = ref[at, :].astype(F32)
                new_left[0, :, at] = BETA_STAT * left[0, :, at] + (1.0 - BETA_STAT) * add
            add = ref[BLOCK : 2 * BLOCK, :].astype(F32)
            new_right[0] = BETA_STAT * right[0] + (1.0 - BETA_STAT) * add


def stats(pos, tab, left, right, grams):
    at = lambda s, pos, tab: (s, 0, 0)
    rows = pl.BlockSpec((1, TILE, BLOCK), at)
    cols = pl.BlockSpec((1, BLOCK, TILE), at)
    fixed = pl.BlockSpec((2 * BLOCK, TILE), lambda s, pos, tab: (0, 0))
    return call(
        stats_body,
        (SLOTS,),
        [rows, cols] + [fixed] * RING,
        [rows, cols],
        [
            jax.ShapeDtypeStruct((SLOTS, TILE, BLOCK), F32),
            jax.ShapeDtypeStruct((SLOTS, BLOCK, TILE), F32),
        ],
        moved=16 * SLOTS * BLOCK * TILE + 16 * BLOCK * TILE,
    )(pos, tab, left, right, *grams)


def back_body(pos, tab, got, step, out):
    for i in range(PER):
        at = rows_at(tab[T_OWNER + RING * i + pos[0]])
        out[ROWS * i : ROWS * (i + 1), :] = got[at, :]
    out[BODY:PIECE, 0:TILE] = step[...]
    out[BODY:PIECE, TILE:HALF] = jnp.zeros((16, HALF - TILE), BF16)


def back(pos, tab, got, step):
    return call(
        back_body,
        (),
        [whole()] * 2,
        whole(),
        jax.ShapeDtypeStruct((PIECE, HALF), BF16),
        moved=2 * (BLOCK + PIECE) * HALF,
    )(pos, tab, got, step)


def place_body(pos, tab, p0, p1, p2, p3, q0, q1, q2, q3, out, vec):
    core = pos[1]
    for k, (ours, theirs) in enumerate(((p0, q0), (p1, q1), (p2, q2), (p3, q3))):
        plane = lax.rem(pos[0] + RING - k, RING)
        for i in range(PER):
            at = rows_at(tab[RING * i + plane])
            out[at, tile_at(core)] = ours[ROWS * i : ROWS * (i + 1), :]
            out[at, tile_at(1 - core)] = theirs[ROWS * i : ROWS * (i + 1), :]

        @pl.when(pl.program_id(0) == 0)
        def _():
            vec[:, tile_at(2 * plane + core)] = ours[BODY:PIECE, :]
            vec[:, tile_at(2 * plane + 1 - core)] = theirs[BODY:PIECE, :]


def place(pos, tab, ours, theirs):
    here = lambda j, pos, tab: (0, j)
    return call(
        place_body,
        (RING,),
        [pl.BlockSpec((PIECE, TILE), here)] * (2 * RING),
        [
            pl.BlockSpec((FULL, CORES * TILE), here),
            pl.BlockSpec((16, BLOCK), lambda j, pos, tab: (0, 0)),
        ],
        [
            jax.ShapeDtypeStruct((FULL, BLOCK), BF16),
            jax.ShapeDtypeStruct((16, BLOCK), BF16),
        ],
        moved=4 * FULL * BLOCK,
    )(pos, tab, *ours, *theirs)


def tables(bucket_block, block_slot, y, owner):
    here = jnp.arange(NBLK, dtype=jnp.int32)
    slot_of = jnp.sum(
        jnp.where(bucket_block[:, None] == here[None, :], block_slot[None, :], 0), axis=1
    )
    rank = jnp.sum((slot_of[None, :] < slot_of[:, None]).astype(jnp.int32), axis=1)
    at_rank = rank[None, :] == here[:, None]
    block = jnp.sum(jnp.where(at_rank, here[None, :], 0), axis=1)
    slot = jnp.sum(jnp.where(at_rank, slot_of[None, :], 0), axis=1)
    holder, local = slot // SLOTS, slot % SLOTS
    ring = jnp.arange(RING, dtype=jnp.int32)
    ours = holder == owner
    sel = jnp.sum(
        jnp.where(
            ours[None, :] & ((here % RING)[None, :] == ((ring + y) % RING)[:, None]),
            local[None, :],
            0,
        ),
        axis=1,
    )
    slots = jnp.arange(SLOTS, dtype=jnp.int32)
    rel = jnp.sum(
        jnp.where(
            ours[None, :] & (local[None, :] == slots[:, None]),
            ((y + RING - here % RING) % RING + 1)[None, :],
            0,
        ),
        axis=1,
    )
    return jnp.concatenate([block, holder, sel, rel - 1]).astype(jnp.int32)


def hop(x, k):
    return lax.ppermute(x, "y", [(i, (i + k) % RING) for i in range(RING)])


def swap(x):
    return lax.ppermute(x, "core", [(0, 1), (1, 0)])


def route(x):
    x = x.reshape(OWNERS, ROWS, HALF)
    return lax.all_to_all(x, ("x", "z"), 0, 0).reshape(BLOCK, HALF)


def shards(
    grads,
    vec_grads,
    factor_left,
    factor_right,
    root_left,
    root_right,
    vec_param,
    vec_first,
    vec_second,
    bucket_block,
    block_slot,
    decay_mask,
):
    y, core = lax.axis_index("y"), lax.axis_index("core")
    owner = lax.axis_index(("x", "z"))
    pos = jnp.stack([y, core]).astype(jnp.int32)
    tab = tables(bucket_block, block_slot, y, owner)
    grad = grads.reshape(FULL, BLOCK)
    vec = jnp.broadcast_to(vec_grads.reshape(1, BLOCK), (16, BLOCK))

    got = swap(pick(pos, pos, grad, vec))
    halves = pair(pos, tab, grad, vec, got)
    root_left, *halves = lax.optimization_barrier((root_left, *halves))
    parts = [halves[0]] + [hop(halves[k], k) for k in range(1, RING)]
    lr = roots(pos, tab, root_left, swap(root_left), root_right)
    send, new_first, new_second, step = total(
        pos, tab, parts, vec_param, vec_first, vec_second, decay_mask
    )
    send, *lr = lax.optimization_barrier((send, *lr))
    lr = [lr[0]] + [hop(lr[k], k) for k in range(1, RING)]
    mine = route(send)
    other = swap(mine)
    result = update(pos, tab, mine, other, lr)
    grams = gram(pos, tab, mine, other)
    result, *grams = lax.optimization_barrier((result, *grams))
    grams = [grams[0]] + [hop(grams[k], k) for k in range(1, RING)]
    piece = back(pos, tab, route(result), step)
    ours = [piece] + [hop(piece, k) for k in range(1, RING)]
    theirs = [swap(x) for x in ours]
    new_left, new_right = stats(pos, tab, factor_left, factor_right, grams)
    block_update, vec_update = place(pos, tab, ours, theirs)
    return (
        block_update.reshape(NBLK, ROWS, BLOCK),
        new_left,
        new_right,
        vec_update[0:1],
        new_first,
        new_second,
    )


def solution(mesh):
    fine = Mesh(mesh.devices.reshape(RING, CORES, 4, 8), ("y", "core", "x", "z"))
    dp, shard = ("y", "core"), ("x", "z")
    return jax.shard_map(
        shards,
        mesh=fine,
        in_specs=(
            P(dp, None, shard, None),
            P(dp, shard, None),
            P(shard, dp, None),
            P(shard, None, dp),
            P(shard, None, dp),
            P(shard, None, dp),
            P(shard, dp),
            P(shard, dp),
            P(shard, dp),
            P(),
            P(),
            P(shard, dp),
        ),
        out_specs=(
            P(None, shard, None),
            P(shard, dp, None),
            P(shard, None, dp),
            P(shard, None),
            P(shard, dp),
            P(shard, dp),
        ),
        check_vma=False,
    )
```

```python
import jax
import jax.numpy as jnp
from jax import lax
from jax.experimental import pallas as pl
from jax.experimental.pallas import tpu as pltpu
from jax.sharding import Mesh
from jax.sharding import PartitionSpec as P

BETA_STAT = 0.95
ADAM_ONE = 0.9
ADAM_TWO = 0.95
ADAM_EPS = 1e-08
DECAY = 0.1

RING = 4
CORES = 2
OWNERS = 32
SLOTS = 3
NBLK = 36
PER = NBLK // RING
BLOCK = 1024
ROWS = BLOCK // OWNERS
TILE = 128
PASS = 256
HALF = BLOCK // CORES
BODY = PER * ROWS
PIECE = BODY + 16
SHARE = 2 * BLOCK + 32
FULL = NBLK * ROWS
BF16 = jnp.bfloat16
F32 = jnp.float32
T_OWNER = 40
T_SEL = 80
T_REL = 84
TABLE = 88
VMEM_LIMIT = 20 * 1024 * 1024


def whole():
    return pl.BlockSpec(memory_space=pltpu.VMEM)


def call(
    body, grid, in_specs, out_specs, out_shape, scratch=(), flops=0, moved=0, limit=VMEM_LIMIT
):
    return pl.pallas_call(
        body,
        name=body.__name__,
        grid_spec=pltpu.PrefetchScalarGridSpec(
            num_scalar_prefetch=2,
            grid=grid,
            in_specs=in_specs,
            out_specs=out_specs,
            scratch_shapes=list(scratch),
        ),
        out_shape=out_shape,
        compiler_params=pltpu.CompilerParams(vmem_limit_bytes=limit),
        cost_estimate=pl.CostEstimate(flops=flops, bytes_accessed=moved, transcendentals=0),
    )


def tile_at(index):
    return pl.ds(pl.multiple_of(index * TILE, TILE), TILE)


def rows_at(index, size=ROWS):
    return pl.ds(pl.multiple_of(index * size, size), size)


def dot(a, b):
    return jnp.dot(a, b, preferred_element_type=F32)


def pair_body(pos, tab, grad, got, vec, got_vec, *outs):
    for k in range(RING):
        plane = lax.rem(pos[0] + k, RING)
        for i in range(PER):
            at = rows_at(tab[RING * i + plane])
            for j in range(RING):
                lanes = tile_at(2 * j + pos[1])
                outs[k][ROWS * i : ROWS * (i + 1), TILE * j : TILE * (j + 1)] = (
                    grad[at, lanes] + got[at, lanes]
                )
        for j in range(RING):
            lanes = tile_at(2 * j + pos[1])
            outs[k][BODY:PIECE, TILE * j : TILE * (j + 1)] = vec[:, lanes] + got_vec[:, lanes]


def pair(pos, tab, grad, got, vec, got_vec):
    return call(
        pair_body,
        (),
        [whole()] * 4,
        [whole()] * RING,
        [jax.ShapeDtypeStruct((PIECE, HALF), BF16)] * RING,
        moved=6 * FULL * HALF,
    )(pos, tab, grad, got, vec, got_vec)


def total_body(pos, tab, a, b, c, d, param, first, second, mask, send, new_first, new_second, step):
    send[...] = jnp.zeros(send.shape, BF16)
    for i in range(PER):
        at = slice(ROWS * i, ROWS * (i + 1))
        total = (a[at, :].astype(F32) + b[at, :].astype(F32)) + (
            c[at, :].astype(F32) + d[at, :].astype(F32)
        )
        send[rows_at(tab[T_OWNER + RING * i + pos[0]]), :] = total.astype(BF16)
    lanes = tile_at(pos[0])
    strips = [ref[BODY:PIECE, lanes].astype(F32) for ref in (a, b, c, d)]
    vec_sum = ((strips[0] + strips[1]) + (strips[2] + strips[3]))[0:1]
    one = ADAM_ONE * first[...] + (1.0 - ADAM_ONE) * vec_sum
    two = ADAM_TWO * second[...] + (1.0 - ADAM_TWO) * vec_sum * vec_sum
    new_first[...] = one
    new_second[...] = two
    update = one / (jnp.sqrt(two) + ADAM_EPS) + DECAY * mask[...].astype(F32) * param[...]
    step[...] = jnp.broadcast_to(update, (16, TILE)).astype(BF16)


def total(pos, tab, parts, param, first, second, mask):
    return call(
        total_body,
        (),
        [whole()] * 8,
        [whole()] * 4,
        [
            jax.ShapeDtypeStruct((BLOCK, HALF), BF16),
            jax.ShapeDtypeStruct((1, TILE), F32),
            jax.ShapeDtypeStruct((1, TILE), F32),
            jax.ShapeDtypeStruct((16, TILE), BF16),
        ],
        moved=8 * PIECE * HALF + 2 * BLOCK * HALF,
    )(pos, tab, *parts, param, first, second, mask)


def roots_body(pos, tab, left, right, *outs):
    for k in range(RING):
        slot = tab[T_SEL + k]
        outs[k][...] = left[slot]
        outs[RING + k][...] = right[slot]


def roots(pos, tab, left, right):
    out = call(
        roots_body,
        (),
        [whole()] * 2,
        [whole()] * (2 * RING),
        [jax.ShapeDtypeStruct((BLOCK, TILE), BF16)] * (2 * RING),
        moved=4 * (SLOTS + RING) * BLOCK * TILE,
    )(pos, tab, left, right)
    return out[:RING], out[RING:]


def update_body(pos, tab, mine, other, *refs):
    ours, theirs, rights = refs[:RING], refs[RING : 2 * RING], refs[2 * RING : 3 * RING]
    out, grad, left, right, applied = refs[3 * RING :]
    core = pos[1]
    for j in range(RING):
        lanes = slice(TILE * j, TILE * (j + 1))
        grad[:, tile_at(2 * j + core)] = mine[:, lanes]
        grad[:, tile_at(2 * j + 1 - core)] = other[:, lanes]
    for k in range(RING):
        plane = lax.rem(pos[0] + RING - k, RING)
        left[:, tile_at(2 * plane + core)] = ours[k][...]
        left[:, tile_at(2 * plane + 1 - core)] = theirs[k][...]
        right[:, tile_at(plane)] = rights[k][...]

    @pl.loop(0, HALF // PASS)
    def _(n):
        at = rows_at(n, PASS)
        applied[:, at] = dot(grad[...], right[:, at]).astype(BF16)

    @pl.loop(0, HALF // PASS)
    def _(n):
        at = rows_at(n, PASS)
        out[:, at] = dot(left[...], applied[:, at]).astype(BF16)


def update(pos, tab, mine, other, ours, theirs, rights):
    return call(
        update_body,
        (),
        [whole()] * (2 + 3 * RING),
        whole(),
        jax.ShapeDtypeStruct((BLOCK, HALF), BF16),
        scratch=[
            pltpu.VMEM((BLOCK, BLOCK), BF16),
            pltpu.VMEM((BLOCK, BLOCK), BF16),
            pltpu.VMEM((BLOCK, HALF), BF16),
            pltpu.VMEM((BLOCK, HALF), BF16),
        ],
        flops=4 * BLOCK * BLOCK * HALF,
        moved=16 * BLOCK * HALF,
    )(pos, tab, mine, other, *ours, *theirs, *rights)


def gram_body(
    pos, tab, mine, other, step, step_other, o0, o1, o2, o3, grad, turned, some, across, down
):
    core = pos[1]
    for j in range(RING):
        lanes = slice(TILE * j, TILE * (j + 1))
        grad[:, tile_at(2 * j + core)] = mine[:, lanes]
        grad[:, tile_at(2 * j + 1 - core)] = other[:, lanes]

    @pl.loop(0, BLOCK // TILE)
    def _(t):
        turned[:, tile_at(t)] = grad[rows_at(t, TILE), :].T

    for j in range(RING):
        some[TILE * j : TILE * (j + 1), :] = grad[rows_at(2 * j + core, TILE), :]

    @pl.loop(0, BLOCK // PASS)
    def _(n):
        at = rows_at(n, PASS)
        across[:, at] = dot(some[...], turned[:, at]).astype(BF16)

    @pl.loop(0, HALF // PASS)
    def _(n):
        at = rows_at(n, PASS)
        down[:, at] = dot(turned[...], mine[:, at]).astype(BF16)

    for k, ref in enumerate((o0, o1, o2, o3)):
        plane = lax.rem(pos[0] + k, RING)
        for t in range(BLOCK // TILE):
            at = slice(TILE * t, TILE * (t + 1))
            ref[at, :] = across[rows_at(plane, TILE), at]
        ref[BLOCK : 2 * BLOCK, :] = down[:, tile_at(plane)]
        ref[2 * BLOCK : 2 * BLOCK + 16, :] = step[...]
        ref[2 * BLOCK + 16 : SHARE, :] = step_other[...]


def gram(pos, tab, mine, other, step, step_other):
    return call(
        gram_body,
        (),
        [whole()] * 4,
        [whole()] * RING,
        [jax.ShapeDtypeStruct((SHARE, TILE), BF16)] * RING,
        scratch=[
            pltpu.VMEM((BLOCK, BLOCK), BF16),
            pltpu.VMEM((BLOCK, BLOCK), BF16),
            pltpu.VMEM((HALF, BLOCK), BF16),
            pltpu.VMEM((HALF, BLOCK), BF16),
            pltpu.VMEM((BLOCK, HALF), BF16),
        ],
        flops=4 * BLOCK * BLOCK * HALF,
        moved=8 * BLOCK * HALF,
    )(pos, tab, mine, other, step, step_other)


def stats_body(pos, tab, left, right, g0, g1, g2, g3, new_left, new_right, vec):
    source = tab[T_REL + pl.program_id(0)]

    @pl.when(source < 0)
    def _():
        new_left[...] = BETA_STAT * left[...]
        new_right[...] = BETA_STAT * right[...]

    @pl.when(pl.program_id(0) == 0)
    def _():
        for k, ref in enumerate((g0, g1, g2, g3)):
            plane = lax.rem(pos[0] + RING - k, RING)
            vec[:, tile_at(2 * plane + pos[1])] = ref[2 * BLOCK : 2 * BLOCK + 16, :]
            vec[:, tile_at(2 * plane + 1 - pos[1])] = ref[2 * BLOCK + 16 : SHARE, :]

    for k, ref in enumerate((g0, g1, g2, g3)):

        @pl.when(source == k)
        def _(ref=ref):
            for t in range(BLOCK // TILE):
                at = slice(TILE * t, TILE * (t + 1))
                add = ref[at, :].astype(F32)
                new_left[0, :, at] = BETA_STAT * left[0, :, at] + (1.0 - BETA_STAT) * add
            add = ref[BLOCK : 2 * BLOCK, :].astype(F32)
            new_right[0] = BETA_STAT * right[0] + (1.0 - BETA_STAT) * add


def stats(pos, tab, left, right, grams):
    at = lambda s, pos, tab: (s, 0, 0)
    rows = pl.BlockSpec((1, TILE, BLOCK), at)
    cols = pl.BlockSpec((1, BLOCK, TILE), at)
    return call(
        stats_body,
        (SLOTS,),
        [rows, cols] + [whole()] * RING,
        [rows, cols, whole()],
        [
            jax.ShapeDtypeStruct((SLOTS, TILE, BLOCK), F32),
            jax.ShapeDtypeStruct((SLOTS, BLOCK, TILE), F32),
            jax.ShapeDtypeStruct((16, BLOCK), BF16),
        ],
        moved=16 * SLOTS * BLOCK * TILE + 16 * BLOCK * TILE,
    )(pos, tab, left, right, *grams)


def back_body(pos, tab, got, out):
    for i in range(PER):
        at = rows_at(tab[T_OWNER + RING * i + pos[0]])
        out[ROWS * i : ROWS * (i + 1), :] = got[at, :]


def back(pos, tab, got):
    return call(
        back_body,
        (),
        [whole()],
        whole(),
        jax.ShapeDtypeStruct((BODY, HALF), BF16),
        moved=2 * (BLOCK + BODY) * HALF,
    )(pos, tab, got)


def place_body(pos, tab, p0, p1, p2, p3, q0, q1, q2, q3, out):
    core = pos[1]
    lanes = tile_at(pl.program_id(0))
    for k, (ours, theirs) in enumerate(((p0, q0), (p1, q1), (p2, q2), (p3, q3))):
        plane = lax.rem(pos[0] + RING - k, RING)
        for i in range(PER):
            at = rows_at(tab[RING * i + plane])
            out[at, tile_at(core)] = ours[ROWS * i : ROWS * (i + 1), lanes]
            out[at, tile_at(1 - core)] = theirs[ROWS * i : ROWS * (i + 1), lanes]


def place(pos, tab, ours, theirs):
    return call(
        place_body,
        (RING,),
        [whole()] * (2 * RING),
        pl.BlockSpec((FULL, CORES * TILE), lambda j, pos, tab: (0, j)),
        jax.ShapeDtypeStruct((FULL, BLOCK), BF16),
        moved=4 * FULL * BLOCK,
    )(pos, tab, *ours, *theirs)


def tables_body(pos, spare, bucket, block_slot, tab, seat, ranks):
    for s in range(OWNERS * SLOTS):
        seat[s] = -1
    for p in range(NBLK):
        seat[block_slot[bucket[p]]] = p
    for k in range(RING):
        tab[T_SEL + k] = 0
    rank = jnp.int32(0)
    for s in range(OWNERS * SLOTS):
        p = seat[s]
        tab[rank] = p
        tab[T_OWNER + rank] = s // SLOTS
        ranks[s] = rank
        rank = rank + jnp.where(p >= 0, 1, 0)
    for k in range(SLOTS):
        s = pos[2] * SLOTS + k
        held = seat[s] >= 0
        plane = lax.rem(ranks[s], RING)
        tab[T_REL + k] = jnp.where(held, lax.rem(pos[0] + RING - plane, RING), -1)
        ahead = T_SEL + lax.rem(plane + RING - pos[0], RING)
        tab[ahead] = jnp.where(held, k, tab[ahead])


def tables(pos, bucket_block, block_slot):
    smem = pl.BlockSpec(memory_space=pltpu.SMEM)
    return call(
        tables_body,
        (),
        [smem] * 2,
        smem,
        jax.ShapeDtypeStruct((TABLE,), jnp.int32),
        scratch=[pltpu.SMEM((OWNERS * SLOTS,), jnp.int32)] * 2,
        moved=2048,
    )(pos, pos, bucket_block, block_slot)


def hop(x, k):
    return lax.ppermute(x, "y", [(i, (i + k) % RING) for i in range(RING)])


def swap(x):
    return lax.ppermute(x, "core", [(0, 1), (1, 0)])


def route(x):
    x = x.reshape(OWNERS, ROWS, HALF)
    return lax.all_to_all(x, ("x", "z"), 0, 0).reshape(BLOCK, HALF)


def shards(
    grads,
    vec_grads,
    factor_left,
    factor_right,
    root_left,
    root_right,
    vec_param,
    vec_first,
    vec_second,
    bucket_block,
    block_slot,
    decay_mask,
):
    y, core = lax.axis_index("y"), lax.axis_index("core")
    owner = lax.axis_index(("x", "z"))
    pos = jnp.stack([y, core, owner]).astype(jnp.int32)
    tab = tables(pos, bucket_block, block_slot)
    grad = grads.reshape(FULL, BLOCK)
    vec = jnp.broadcast_to(vec_grads.reshape(1, BLOCK), (16, BLOCK))

    got, got_vec = swap(grad), swap(vec)
    halves = pair(pos, tab, grad, got, vec, got_vec)
    parts = [halves[0]] + [hop(halves[k], k) for k in range(1, RING)]
    lefts, rights = roots(pos, tab, root_left, root_right)
    parts, lefts, rights = lax.optimization_barrier((parts, lefts, rights))
    send, new_first, new_second, step = total(
        pos, tab, parts, vec_param, vec_first, vec_second, decay_mask
    )
    send, lefts, rights = lax.optimization_barrier((send, lefts, rights))
    lefts = [lefts[0]] + [hop(lefts[k], k) for k in range(1, RING)]
    rights = [rights[0]] + [hop(rights[k], k) for k in range(1, RING)]
    mine = route(send)
    mine, lefts, rights = lax.optimization_barrier((mine, lefts, rights))
    other = swap(mine)
    others = [swap(x) for x in lefts]
    result = update(pos, tab, mine, other, lefts, others, rights)
    result, mine, other = lax.optimization_barrier((result, mine, other))
    grams = gram(pos, tab, mine, other, step, swap(step))
    grams = [grams[0]] + [hop(grams[k], k) for k in range(1, RING)]
    got = route(result)
    got, *grams = lax.optimization_barrier((got, *grams))
    piece = back(pos, tab, got)
    ours = [piece] + [hop(piece, k) for k in range(1, RING)]
    new_left, new_right, vec_update = stats(pos, tab, factor_left, factor_right, grams)
    ours[3], new_left, new_right = lax.optimization_barrier((ours[3], new_left, new_right))
    theirs = [swap(x) for x in ours]
    block_update = place(pos, tab, ours, theirs)
    return (
        block_update.reshape(NBLK, ROWS, BLOCK),
        new_left,
        new_right,
        vec_update[0:1],
        new_first,
        new_second,
    )


def solution(mesh):
    fine = Mesh(mesh.devices.reshape(RING, CORES, 4, 8), ("y", "core", "x", "z"))
    dp, shard = ("y", "core"), ("x", "z")
    return jax.shard_map(
        shards,
        mesh=fine,
        in_specs=(
            P(dp, None, shard, None),
            P(dp, shard, None),
            P(shard, dp, None),
            P(shard, None, dp),
            P(shard, None, dp),
            P(shard, None, dp),
            P(shard, dp),
            P(shard, dp),
            P(shard, dp),
            P(),
            P(),
            P(shard, dp),
        ),
        out_specs=(
            P(None, shard, None),
            P(shard, dp, None),
            P(shard, None, dp),
            P(shard, None),
            P(shard, dp),
            P(shard, dp),
        ),
        check_vma=False,
    )
```

```python
import jax
import jax.numpy as jnp
from jax import lax
from jax.experimental import pallas as pl
from jax.experimental.pallas import tpu as pltpu
from jax.sharding import Mesh
from jax.sharding import PartitionSpec as P

BETA_STAT = 0.95
ADAM_ONE = 0.9
ADAM_TWO = 0.95
ADAM_EPS = 1e-08
DECAY = 0.1

RING = 4
CORES = 2
OWNERS = 32
SLOTS = 3
NBLK = 36
PER = NBLK // RING
BLOCK = 1024
ROWS = BLOCK // OWNERS
TILE = 128
PASS = 512
HALF = BLOCK // CORES
BODY = PER * ROWS
PIECE = BODY + 16
SHARE = 2 * BLOCK + 32
FULL = NBLK * ROWS
BF16 = jnp.bfloat16
F32 = jnp.float32
T_OWNER = 40
T_SEL = 80
T_REL = 84
TABLE = 88
VMEM_LIMIT = 24 * 1024 * 1024


def whole():
    return pl.BlockSpec(memory_space=pltpu.VMEM)


def call(
    body, grid, in_specs, out_specs, out_shape, scratch=(), flops=0, moved=0, limit=VMEM_LIMIT
):
    return pl.pallas_call(
        body,
        name=body.__name__,
        grid_spec=pltpu.PrefetchScalarGridSpec(
            num_scalar_prefetch=2,
            grid=grid,
            in_specs=in_specs,
            out_specs=out_specs,
            scratch_shapes=list(scratch),
        ),
        out_shape=out_shape,
        compiler_params=pltpu.CompilerParams(vmem_limit_bytes=limit),
        cost_estimate=pl.CostEstimate(flops=flops, bytes_accessed=moved, transcendentals=0),
    )


def outside():
    return pl.BlockSpec(memory_space=pltpu.HBM)


def stay(x):
    return jax.tree.map(lambda a: pltpu.with_memory_space_constraint(a, pltpu.HBM), x)


def tile_at(index):
    return pl.ds(pl.multiple_of(index * TILE, TILE), TILE)


def rows_at(index, size=ROWS):
    return pl.ds(pl.multiple_of(index * size, size), size)


def dot(a, b):
    return jnp.dot(a, b, preferred_element_type=F32)


def half_body(pos, spare, grad, own, sems):
    copies = [
        pltpu.make_async_copy(grad.at[:, tile_at(2 * j + pos[1])], own.at[j], sems.at[j])
        for j in range(RING)
    ]
    for copy in copies:
        copy.start()
    for copy in copies:
        copy.wait()


def half(pos, grad):
    return call(
        half_body,
        (),
        [outside()],
        whole(),
        jax.ShapeDtypeStruct((RING, FULL, TILE), BF16),
        scratch=[pltpu.SemaphoreType.DMA((RING,))],
        moved=4 * FULL * HALF,
    )(pos, pos, stay(grad))


def pair_body(pos, tab, own, got, vec, got_vec, h0, h1, h2, h3):
    lanes_of = [tile_at(2 * j + pos[1]) for j in range(RING)]
    for k, out in enumerate((h0, h1, h2, h3)):
        plane = lax.rem(pos[0] + k, RING)
        for i in range(PER):
            at = rows_at(tab[RING * i + plane])
            for j, lanes in enumerate(lanes_of):
                here = slice(TILE * j, TILE * (j + 1))
                out[ROWS * i : ROWS * (i + 1), here] = own[j, at, :] + got[at, lanes]
    for j, lanes in enumerate(lanes_of):
        both = vec[0, :, lanes].astype(F32) + got_vec[0, :, lanes].astype(F32)
        strip = jnp.broadcast_to(both, (16, TILE)).astype(BF16)
        for out in (h0, h1, h2, h3):
            out[BODY:PIECE, TILE * j : TILE * (j + 1)] = strip


def pair(pos, tab, own, got, vec, got_vec):
    return call(
        pair_body,
        (),
        [whole()] * 4,
        [whole()] * RING,
        [jax.ShapeDtypeStruct((PIECE, HALF), BF16)] * RING,
        moved=6 * FULL * HALF,
    )(pos, tab, own, got, stay(vec), got_vec)


def total_body(pos, tab, a, b, c, d, param, first, second, mask, send, new_first, new_second, step):
    send[...] = jnp.zeros(send.shape, BF16)
    for i in range(PER):
        at = slice(ROWS * i, ROWS * (i + 1))
        total = (a[at, :].astype(F32) + b[at, :].astype(F32)) + (
            c[at, :].astype(F32) + d[at, :].astype(F32)
        )
        send[rows_at(tab[T_OWNER + RING * i + pos[0]]), :] = total.astype(BF16)
    lanes = tile_at(pos[0])
    strips = [ref[BODY:PIECE, lanes].astype(F32) for ref in (a, b, c, d)]
    vec_sum = ((strips[0] + strips[1]) + (strips[2] + strips[3]))[0:1]
    one = ADAM_ONE * first[...] + (1.0 - ADAM_ONE) * vec_sum
    two = ADAM_TWO * second[...] + (1.0 - ADAM_TWO) * vec_sum * vec_sum
    new_first[...] = one
    new_second[...] = two
    update = one / (jnp.sqrt(two) + ADAM_EPS) + DECAY * mask[...].astype(F32) * param[...]
    step[...] = jnp.broadcast_to(update, (16, TILE)).astype(BF16)


def total(pos, tab, parts, param, first, second, mask):
    return call(
        total_body,
        (),
        [whole()] * 8,
        [whole()] * 4,
        [
            pltpu.HBM((BLOCK, HALF), BF16),
            jax.ShapeDtypeStruct((1, TILE), F32),
            jax.ShapeDtypeStruct((1, TILE), F32),
            jax.ShapeDtypeStruct((16, TILE), BF16),
        ],
        moved=8 * PIECE * HALF + 2 * BLOCK * HALF,
    )(pos, tab, *parts, param, first, second, mask)


def roots_body(pos, tab, left, right, *outs):
    for k in range(RING):
        slot = tab[T_SEL + k]
        outs[k][0:BLOCK, :] = left[slot]
        for j in range(RING):
            for n, tile in enumerate((2 * j + pos[1], 2 * j + 1 - pos[1])):
                at = BLOCK + HALF * n + TILE * j
                outs[k][at : at + TILE, :] = right[slot, rows_at(tile, TILE), :]


def roots(pos, tab, left, right):
    return call(
        roots_body,
        (),
        [whole()] * 2,
        [whole()] * RING,
        [pltpu.HBM((2 * BLOCK, TILE), BF16)] * RING,
        moved=4 * (SLOTS + RING) * BLOCK * TILE,
    )(pos, tab, left, right)


def update_body(pos, tab, mine, other, *refs):
    ours, theirs = refs[:RING], refs[RING : 2 * RING]
    out, left, right, applied, result, sems, out_sems = refs[2 * RING :]
    core = pos[1]
    copies = [[], [], []]
    for k in range(RING):
        plane = lax.rem(pos[0] + RING - k, RING)
        targets = (
            (ours[k].at[BLOCK : 2 * BLOCK, :], right.at[:, tile_at(plane)]),
            (ours[k].at[0:BLOCK, :], left.at[:, tile_at(2 * plane + core)]),
            (theirs[k].at[0:BLOCK, :], left.at[:, tile_at(2 * plane + 1 - core)]),
        )
        for n, (ref, buf) in enumerate(targets):
            copies[n].append(pltpu.make_async_copy(ref, buf, sems.at[n, k]))
    for group in copies:
        for copy in group:
            copy.start()
    for copy in copies[0]:
        copy.wait()
    applied[...] = (
        dot(mine[...], right[0:HALF, :]) + dot(other[...], right[HALF:BLOCK, :])
    ).astype(BF16)
    for copy in copies[1] + copies[2]:
        copy.wait()
    stores = []
    for n in range(BLOCK // PASS):
        at = slice(PASS * n, PASS * (n + 1))
        result[at, :] = dot(left[at, :], applied[...]).astype(BF16)
        stores.append(pltpu.make_async_copy(result.at[at, :], out.at[at, :], out_sems.at[n]))
        stores[n].start()
    for copy in stores:
        copy.wait()


def update(pos, tab, mine, other, ours, theirs):
    return call(
        update_body,
        (),
        [whole()] * 2 + [outside()] * (2 * RING),
        outside(),
        pltpu.HBM((BLOCK, HALF), BF16),
        scratch=[
            pltpu.VMEM((BLOCK, BLOCK), BF16),
            pltpu.VMEM((BLOCK, HALF), BF16),
            pltpu.VMEM((BLOCK, HALF), BF16),
            pltpu.VMEM((BLOCK, HALF), BF16),
            pltpu.SemaphoreType.DMA((3, RING)),
            pltpu.SemaphoreType.DMA((BLOCK // PASS,)),
        ],
        flops=4 * BLOCK * BLOCK * HALF,
        moved=16 * BLOCK * HALF,
    )(pos, tab, mine, other, *stay(ours), *theirs)


def turn(core, buf, turned, some):
    for j in range(RING):
        at = slice(TILE * j, TILE * (j + 1))
        turned[at, :] = buf[:, at].T
        some[at, :] = buf[rows_at(2 * j + core, TILE), :]


def gram_first_body(pos, tab, mine, across, down, turned, some):
    turn(pos[1], mine, turned, some)
    across[...] = dot(some[...], turned[...])
    down[...] = dot(turned[...], mine[...]).astype(BF16)


def gram_first(pos, tab, mine):
    return call(
        gram_first_body,
        (),
        [whole()],
        [whole()] * 2,
        [
            jax.ShapeDtypeStruct((HALF, BLOCK), F32),
            jax.ShapeDtypeStruct((HALF, HALF), BF16),
        ],
        scratch=[pltpu.VMEM((HALF, BLOCK), BF16), pltpu.VMEM((HALF, HALF), BF16)],
        flops=2 * BLOCK * BLOCK * HALF,
        moved=4 * BLOCK * BLOCK,
    )(pos, tab, mine)


def gram_body(
    pos, tab, mine, other, half, down, step, step_other, o0, o1, o2, o3, turned, some, across, down_other, held, sems
):
    core = pos[1]
    outs = (o0, o1, o2, o3)
    copies = []

    def send(k, n, low, high):
        copy = pltpu.make_async_copy(
            held.at[k, low:high, :], outs[k].at[low:high, :], sems.at[k, n]
        )
        copy.start()
        copies.append(copy)

    turn(core, other, turned, some)
    across[...] = (half[...] + dot(some[...], turned[...])).astype(BF16)
    for k in range(RING):
        plane = lax.rem(pos[0] + k, RING)
        for t in range(BLOCK // TILE):
            at = slice(TILE * t, TILE * (t + 1))
            held[k, at, :] = across[rows_at(plane, TILE), at]
        send(k, 0, 0, BLOCK)
    down_other[...] = dot(turned[...], mine[...]).astype(BF16)
    for k in range(RING):
        plane = lax.rem(pos[0] + k, RING)
        for j in range(RING):
            at = slice(TILE * j, TILE * (j + 1))
            lanes = tile_at(plane)
            held[k, rows_at(BLOCK // TILE + 2 * j + core, TILE), :] = down[at, lanes]
            held[k, rows_at(BLOCK // TILE + 2 * j + 1 - core, TILE), :] = down_other[at, lanes]
        held[k, 2 * BLOCK : 2 * BLOCK + 16, :] = step[...]
        held[k, 2 * BLOCK + 16 : SHARE, :] = step_other[...]
        send(k, 1, BLOCK, SHARE)
    for copy in copies:
        copy.wait()


def gram(pos, tab, mine, other, half, down, step, step_other):
    return call(
        gram_body,
        (),
        [whole()] * 6,
        [outside()] * RING,
        [pltpu.HBM((SHARE, TILE), BF16)] * RING,
        scratch=[
            pltpu.VMEM((HALF, BLOCK), BF16),
            pltpu.VMEM((HALF, HALF), BF16),
            pltpu.VMEM((HALF, BLOCK), BF16),
            pltpu.VMEM((HALF, HALF), BF16),
            pltpu.VMEM((RING, SHARE, TILE), BF16),
            pltpu.SemaphoreType.DMA((RING, 2)),
        ],
        flops=2 * BLOCK * BLOCK * HALF,
        moved=8 * BLOCK * HALF,
    )(pos, tab, mine, other, half, down, step, step_other)


def stats_body(
    pos, tab, left, right, g0, g1, g2, g3, new_left, new_right, vec, rows, cols, held, sems, gram_sems
):
    gets = [pltpu.make_async_copy(g, held.at[k], gram_sems.at[k]) for k, g in enumerate((g0, g1, g2, g3))]
    loads, stores = [], []
    for s in range(SLOTS):
        pairs = ((left, rows, new_left), (right, cols, new_right))
        loads += [
            pltpu.make_async_copy(a.at[s], b.at[s], sems.at[0, s, n])
            for n, (a, b, c) in enumerate(pairs)
        ]
        stores += [
            pltpu.make_async_copy(b.at[s], c.at[s], sems.at[1, s, n])
            for n, (a, b, c) in enumerate(pairs)
        ]
    for copy in gets + loads:
        copy.start()
    for k in range(RING):
        gets[k].wait()
        plane = lax.rem(pos[0] + RING - k, RING)
        vec[:, tile_at(2 * plane + pos[1])] = held[k, 2 * BLOCK : 2 * BLOCK + 16, :]
        vec[:, tile_at(2 * plane + 1 - pos[1])] = held[k, 2 * BLOCK + 16 : SHARE, :]
    for s in range(SLOTS):
        source = tab[T_REL + s]
        some = source >= 0
        k = jnp.maximum(source, 0)
        loads[2 * s].wait()
        for t in range(BLOCK // TILE):
            at = slice(TILE * t, TILE * (t + 1))
            add = jnp.where(some, held[k, at, :].astype(F32), 0.0)
            rows[s, :, at] = BETA_STAT * rows[s, :, at] + (1.0 - BETA_STAT) * add
        stores[2 * s].start()
        loads[2 * s + 1].wait()
        add = jnp.where(some, held[k, BLOCK : 2 * BLOCK, :].astype(F32), 0.0)
        cols[s] = BETA_STAT * cols[s] + (1.0 - BETA_STAT) * add
        stores[2 * s + 1].start()
    for copy in stores:
        copy.wait()


def stats(pos, tab, left, right, grams):
    return call(
        stats_body,
        (),
        [outside()] * (2 + RING),
        [outside(), outside(), whole()],
        [
            jax.ShapeDtypeStruct((SLOTS, TILE, BLOCK), F32),
            jax.ShapeDtypeStruct((SLOTS, BLOCK, TILE), F32),
            jax.ShapeDtypeStruct((16, BLOCK), BF16),
        ],
        scratch=[
            pltpu.VMEM((SLOTS, TILE, BLOCK), F32),
            pltpu.VMEM((SLOTS, BLOCK, TILE), F32),
            pltpu.VMEM((RING, SHARE, TILE), BF16),
            pltpu.SemaphoreType.DMA((2, SLOTS, 2)),
            pltpu.SemaphoreType.DMA((RING,)),
        ],
        moved=16 * SLOTS * BLOCK * TILE + 16 * BLOCK * TILE,
    )(pos, tab, *stay([left, right, *grams]))


def back_body(pos, tab, got, out):
    for i in range(PER):
        at = rows_at(tab[T_OWNER + RING * i + pos[0]])
        out[ROWS * i : ROWS * (i + 1), :] = got[at, :]


def back(pos, tab, got):
    return call(
        back_body,
        (),
        [whole()],
        whole(),
        jax.ShapeDtypeStruct((BODY, HALF), BF16),
        moved=2 * (BLOCK + BODY) * HALF,
    )(pos, tab, got)


def place_body(hops, pos, tab, *refs):
    out, rows, sems = refs[-3:]
    core = pos[1]
    copies = []
    for n, k in enumerate(hops):
        plane = lax.rem(pos[0] + RING - k, RING)
        ours, theirs = refs[2 * n], refs[2 * n + 1]
        for i in range(PER):
            at = slice(ROWS * i, ROWS * (i + 1))
            slab = n * PER + i
            here = slice(ROWS * slab, ROWS * (slab + 1))
            for j in range(RING):
                lanes = slice(TILE * j, TILE * (j + 1))
                rows[here, tile_at(2 * j + core)] = ours[at, lanes]
                rows[here, tile_at(2 * j + 1 - core)] = theirs[at, lanes]
            target = out.at[rows_at(tab[RING * i + plane]), :]
            copies.append(pltpu.make_async_copy(rows.at[here, :], target, sems.at[slab]))
            copies[-1].start()
    for copy in copies:
        copy.wait()


def place(pos, tab, hops, parts, onto=None):
    def place_part(*refs):
        place_body(hops, *refs)

    slabs = PER * len(hops)
    extra = () if onto is None else (onto,)
    return pl.pallas_call(
        place_part,
        name="place_part",
        grid_spec=pltpu.PrefetchScalarGridSpec(
            num_scalar_prefetch=2,
            grid=(),
            in_specs=[whole()] * (2 * len(hops)) + [outside()] * len(extra),
            out_specs=outside(),
            scratch_shapes=[
                pltpu.VMEM((ROWS * slabs, BLOCK), BF16),
                pltpu.SemaphoreType.DMA((slabs,)),
            ],
        ),
        out_shape=jax.ShapeDtypeStruct((FULL, BLOCK), BF16),
        input_output_aliases={} if onto is None else {2 + 2 * len(hops): 0},
        compiler_params=pltpu.CompilerParams(vmem_limit_bytes=VMEM_LIMIT),
        cost_estimate=pl.CostEstimate(
            flops=0, bytes_accessed=4 * ROWS * slabs * BLOCK, transcendentals=0
        ),
    )(pos, tab, *parts, *extra)


def tables_body(pos, spare, maps, tab, seat, ranks):
    for s in range(OWNERS * SLOTS):
        seat[s] = -1
    for p in range(NBLK):
        seat[maps[NBLK + maps[p]]] = p
    for k in range(RING):
        tab[T_SEL + k] = 0
    rank = jnp.int32(0)
    for s in range(OWNERS * SLOTS):
        p = seat[s]
        tab[rank] = p
        tab[T_OWNER + rank] = s // SLOTS
        ranks[s] = rank
        rank = rank + jnp.where(p >= 0, 1, 0)
    for k in range(SLOTS):
        s = pos[2] * SLOTS + k
        held = seat[s] >= 0
        plane = lax.rem(ranks[s], RING)
        tab[T_REL + k] = jnp.where(held, lax.rem(pos[0] + RING - plane, RING), -1)
        ahead = T_SEL + lax.rem(plane + RING - pos[0], RING)
        tab[ahead] = jnp.where(held, k, tab[ahead])


def tables(pos, bucket_block, block_slot):
    smem = pl.BlockSpec(memory_space=pltpu.SMEM)
    return call(
        tables_body,
        (),
        [smem],
        smem,
        jax.ShapeDtypeStruct((TABLE,), jnp.int32),
        scratch=[pltpu.SMEM((OWNERS * SLOTS,), jnp.int32)] * 2,
        moved=2048,
    )(pos, pos, jnp.concatenate([bucket_block, block_slot]))


def hop(x, k):
    return lax.ppermute(x, "y", [(i, (i + k) % RING) for i in range(RING)])


def swap(x):
    return lax.ppermute(x, "core", [(0, 1), (1, 0)])


def route(x):
    x = x.reshape(OWNERS, ROWS, HALF)
    return lax.all_to_all(x, ("x", "z"), 0, 0).reshape(BLOCK, HALF)


def shards(
    grads,
    vec_grads,
    factor_left,
    factor_right,
    root_left,
    root_right,
    vec_param,
    vec_first,
    vec_second,
    bucket_block,
    block_slot,
    decay_mask,
):
    y, core = lax.axis_index("y"), lax.axis_index("core")
    owner = lax.axis_index(("x", "z"))
    pos = jnp.stack([y, core, owner]).astype(jnp.int32)
    tab = tables(pos, bucket_block, block_slot)
    grad = grads.reshape(FULL, BLOCK)

    got, got_vec = swap(grad), swap(vec_grads)
    halves = pair(pos, tab, half(pos, grad), got, vec_grads, got_vec)
    parts = [halves[0]] + [hop(halves[k], k) for k in range(1, RING)]
    sides = roots(pos, tab, root_left, root_right)
    parts, sides = lax.optimization_barrier((parts, sides))
    send, new_first, new_second, step = total(
        pos, tab, parts, vec_param, vec_first, vec_second, decay_mask
    )
    send, sides = lax.optimization_barrier((send, sides))
    sides = [sides[0]] + [hop(sides[k], k) for k in range(1, RING)]
    mine = route(send)
    step_other = swap(step)
    mine, sides, step_other = lax.optimization_barrier((mine, sides, step_other))
    other = swap(mine)
    first = gram_first(pos, tab, mine)
    other, sides, first = lax.optimization_barrier((other, sides, first))
    grams = gram(pos, tab, mine, other, *first, step, step_other)
    others = [swap(x) for x in sides]
    others, grams = lax.optimization_barrier((others, grams))
    result = update(pos, tab, mine, other, sides, others)
    result, grams = lax.optimization_barrier((result, grams))
    grams = [grams[0]] + [hop(grams[k], k) for k in range(1, RING)]
    got = route(result)
    got, *grams = lax.optimization_barrier((got, *grams))
    piece = back(pos, tab, got)
    ours = [piece] + [hop(piece, k) for k in range(1, RING)]
    new_left, new_right, vec_update = stats(pos, tab, factor_left, factor_right, grams)
    ours[3], new_left, new_right, vec_update = lax.optimization_barrier(
        (ours[3], new_left, new_right, vec_update[0:1])
    )
    both = [[x, swap(x)] for x in (ours[0], ours[3], ours[2])]
    placed = place(pos, tab, (0, 3, 2), both[0] + both[1] + both[2])
    block_update = place(pos, tab, (1,), [ours[1], swap(ours[1])], placed)
    return (
        block_update.reshape(NBLK, ROWS, BLOCK),
        new_left,
        new_right,
        vec_update,
        new_first,
        new_second,
    )


def solution(mesh):
    fine = Mesh(mesh.devices.reshape(RING, CORES, 4, 8), ("y", "core", "x", "z"))
    dp, shard = ("y", "core"), ("x", "z")
    return jax.shard_map(
        shards,
        mesh=fine,
        in_specs=(
            P(dp, None, shard, None),
            P(dp, shard, None),
            P(shard, dp, None),
            P(shard, None, dp),
            P(shard, None, dp),
            P(shard, None, dp),
            P(shard, dp),
            P(shard, dp),
            P(shard, dp),
            P(),
            P(),
            P(shard, dp),
        ),
        out_specs=(
            P(None, shard, None),
            P(shard, dp, None),
            P(shard, None, dp),
            P(shard, None),
            P(shard, dp),
            P(shard, dp),
        ),
        check_vma=False,
    )
```

```python
import jax
import jax.numpy as jnp
from jax import lax
from jax.experimental import pallas as pl
from jax.experimental.pallas import tpu as pltpu
from jax.sharding import Mesh
from jax.sharding import PartitionSpec as P

BETA_STAT = 0.95
ADAM_ONE = 0.9
ADAM_TWO = 0.95
ADAM_EPS = 1e-08
DECAY = 0.1

RING = 4
CORES = 2
OWNERS = 32
SLOTS = 3
NBLK = 36
PER = NBLK // RING
BLOCK = 1024
ROWS = BLOCK // OWNERS
TILE = 128
PASS = 512
HALF = BLOCK // CORES
BODY = PER * ROWS
HEAD = (PER + 1) // 2
A_ROWS = HEAD * ROWS
B_ROWS = BODY - A_ROWS
BS_ROWS = B_ROWS + 16
SHARE = 2 * BLOCK + 32
FULL = NBLK * ROWS
BF16 = jnp.bfloat16
F32 = jnp.float32
T_OWNER = 40
T_SEL = 80
T_REL = 84
TABLE = 88
VMEM_LIMIT = 24 * 1024 * 1024


def whole():
    return pl.BlockSpec(memory_space=pltpu.VMEM)


def call(
    body, grid, in_specs, out_specs, out_shape, scratch=(), flops=0, moved=0, limit=VMEM_LIMIT
):
    return pl.pallas_call(
        body,
        name=body.__name__,
        grid_spec=pltpu.PrefetchScalarGridSpec(
            num_scalar_prefetch=2,
            grid=grid,
            in_specs=in_specs,
            out_specs=out_specs,
            scratch_shapes=list(scratch),
        ),
        out_shape=out_shape,
        compiler_params=pltpu.CompilerParams(vmem_limit_bytes=limit),
        cost_estimate=pl.CostEstimate(flops=flops, bytes_accessed=moved, transcendentals=0),
    )


def outside():
    return pl.BlockSpec(memory_space=pltpu.HBM)


def stay(x):
    return jax.tree.map(lambda a: pltpu.with_memory_space_constraint(a, pltpu.HBM), x)


def tile_at(index):
    return pl.ds(pl.multiple_of(index * TILE, TILE), TILE)


def rows_at(index, size=ROWS):
    return pl.ds(pl.multiple_of(index * size, size), size)


def dot(a, b):
    return jnp.dot(a, b, preferred_element_type=F32)


def front_body(pos, spare, maps, grad, tab, own, seat, ranks, sems):
    copies = [
        pltpu.make_async_copy(grad.at[:, tile_at(2 * j + pos[1])], own.at[j], sems.at[j])
        for j in range(RING)
    ]
    for copy in copies:
        copy.start()
    for s in range(OWNERS * SLOTS):
        seat[s] = -1
    for p in range(NBLK):
        seat[maps[NBLK + maps[p]]] = p
    for k in range(RING):
        tab[T_SEL + k] = 0
    rank = jnp.int32(0)
    for s in range(OWNERS * SLOTS):
        p = seat[s]
        tab[rank] = p
        tab[T_OWNER + rank] = s // SLOTS
        ranks[s] = rank
        rank = rank + jnp.where(p >= 0, 1, 0)
    for k in range(SLOTS):
        s = pos[2] * SLOTS + k
        held = seat[s] >= 0
        plane = lax.rem(ranks[s], RING)
        tab[T_REL + k] = jnp.where(held, lax.bitwise_xor(pos[0], plane), -1)
        ahead = T_SEL + lax.bitwise_xor(pos[0], plane)
        tab[ahead] = jnp.where(held, k, tab[ahead])
    for copy in copies:
        copy.wait()


def front(pos, maps, grad):
    smem = pl.BlockSpec(memory_space=pltpu.SMEM)
    return call(
        front_body,
        (),
        [smem, outside()],
        [smem, whole()],
        [
            jax.ShapeDtypeStruct((TABLE,), jnp.int32),
            jax.ShapeDtypeStruct((RING, FULL, TILE), BF16),
        ],
        scratch=[
            pltpu.SMEM((OWNERS * SLOTS,), jnp.int32),
            pltpu.SMEM((OWNERS * SLOTS,), jnp.int32),
            pltpu.SemaphoreType.DMA((RING,)),
        ],
        moved=4 * FULL * HALF,
    )(pos, pos, maps, stay(grad))


def pair_body(pos, tab, own, got, vec, got_vec, give_a, keep_a, give_b, keep_b):
    lanes_of = [tile_at(2 * j + pos[1]) for j in range(RING)]
    first = {0: (keep_a, 0), 3: (keep_a, 1), 1: (give_a, 0), 2: (give_a, 1)}
    second = {0: (keep_b, 0), 1: (keep_b, 1), 3: (give_b, 0), 2: (give_b, 1)}
    for k in range(RING):
        plane = lax.bitwise_xor(pos[0], k)
        for i in range(PER):
            at = rows_at(tab[RING * i + plane])
            out, part = first[k] if i < HEAD else second[k]
            low = part * A_ROWS + ROWS * i if i < HEAD else part * BS_ROWS + ROWS * (i - HEAD)
            for j, lanes in enumerate(lanes_of):
                here = slice(TILE * j, TILE * (j + 1))
                out[low : low + ROWS, here] = own[j, at, :] + got[at, lanes]
    for j, lanes in enumerate(lanes_of):
        both = vec[0, :, lanes].astype(F32) + got_vec[0, :, lanes].astype(F32)
        strip = jnp.broadcast_to(both, (16, TILE)).astype(BF16)
        for out, part in second.values():
            low = part * BS_ROWS + B_ROWS
            out[low : low + 16, TILE * j : TILE * (j + 1)] = strip


def pair(pos, tab, own, got, vec, got_vec):
    return call(
        pair_body,
        (),
        [whole()] * 4,
        [whole()] * 4,
        [jax.ShapeDtypeStruct((2 * n, HALF), BF16) for n in (A_ROWS, A_ROWS, BS_ROWS, BS_ROWS)],
        moved=6 * FULL * HALF,
    )(pos, tab, own, got, stay(vec), got_vec)


def total_body(
    pos, tab, a0, a1, a2, b0, b1, b2, param, first, second, mask, send, new_first, new_second, step
):
    send[...] = jnp.zeros(send.shape, BF16)
    for i in range(PER):
        refs, low = ((a0, a1, a2), ROWS * i) if i < HEAD else ((b0, b1, b2), ROWS * (i - HEAD))
        parts = [ref[low : low + ROWS, :].astype(F32) for ref in refs]
        total = (parts[0] + parts[1]) + parts[2]
        send[rows_at(tab[T_OWNER + RING * i + pos[0]]), :] = total.astype(BF16)
    strips = [ref[B_ROWS:BS_ROWS, tile_at(pos[0])].astype(F32) for ref in (b0, b1, b2)]
    vec_sum = ((strips[0] + strips[1]) + strips[2])[0:1]
    one = ADAM_ONE * first[...] + (1.0 - ADAM_ONE) * vec_sum
    two = ADAM_TWO * second[...] + (1.0 - ADAM_TWO) * vec_sum * vec_sum
    new_first[...] = one
    new_second[...] = two
    update = one / (jnp.sqrt(two) + ADAM_EPS) + DECAY * mask[...].astype(F32) * param[...]
    step[...] = jnp.broadcast_to(update, (16, TILE)).astype(BF16)


def total(pos, tab, parts, param, first, second, mask):
    return call(
        total_body,
        (),
        [whole()] * 10,
        [whole()] * 4,
        [
            pltpu.HBM((BLOCK, HALF), BF16),
            jax.ShapeDtypeStruct((1, TILE), F32),
            jax.ShapeDtypeStruct((1, TILE), F32),
            jax.ShapeDtypeStruct((16, TILE), BF16),
        ],
        moved=12 * BODY * HALF + 2 * BLOCK * HALF,
    )(pos, tab, *parts, param, first, second, mask)


def roots_body(pos, tab, left, right, *outs):
    for k in range(RING):
        slot = tab[T_SEL + k]
        outs[k][0:BLOCK, :] = left[slot]
        for j in range(RING):
            for n, tile in enumerate((2 * j + pos[1], 2 * j + 1 - pos[1])):
                at = BLOCK + HALF * n + TILE * j
                outs[k][at : at + TILE, :] = right[slot, rows_at(tile, TILE), :]


def roots(pos, tab, left, right):
    return call(
        roots_body,
        (),
        [whole()] * 2,
        [whole()] * RING,
        [pltpu.HBM((2 * BLOCK, TILE), BF16)] * RING,
        moved=4 * (SLOTS + RING) * BLOCK * TILE,
    )(pos, tab, left, right)


def update_body(pos, tab, mine, other, right, *refs):
    ours, theirs = refs[:RING], refs[RING : 2 * RING]
    out, left, applied, result, sems, out_sems = refs[2 * RING :]
    core = pos[1]
    copies = []
    for k in range(RING):
        plane = lax.bitwise_xor(pos[0], k)
        for n, (ref, tile) in enumerate(((ours[k], 2 * plane + core), (theirs[k], 2 * plane + 1 - core))):
            copies.append(
                pltpu.make_async_copy(ref.at[0:BLOCK, :], left.at[:, tile_at(tile)], sems.at[n, k])
            )
    for copy in copies:
        copy.start()
    applied[...] = (
        dot(mine[...], right[0:HALF, :]) + dot(other[...], right[HALF:BLOCK, :])
    ).astype(BF16)
    for copy in copies:
        copy.wait()
    stores = []
    for n in range(BLOCK // PASS):
        at = slice(PASS * n, PASS * (n + 1))
        result[at, :] = dot(left[at, :], applied[...]).astype(BF16)
        stores.append(pltpu.make_async_copy(result.at[at, :], out.at[at, :], out_sems.at[n]))
        stores[n].start()
    for copy in stores:
        copy.wait()


def update(pos, tab, mine, other, right, ours, theirs):
    return call(
        update_body,
        (),
        [whole()] * 3 + [outside()] * (2 * RING),
        outside(),
        pltpu.HBM((BLOCK, HALF), BF16),
        scratch=[
            pltpu.VMEM((BLOCK, BLOCK), BF16),
            pltpu.VMEM((BLOCK, HALF), BF16),
            pltpu.VMEM((BLOCK, HALF), BF16),
            pltpu.SemaphoreType.DMA((2, RING)),
            pltpu.SemaphoreType.DMA((BLOCK // PASS,)),
        ],
        flops=4 * BLOCK * BLOCK * HALF,
        moved=16 * BLOCK * HALF,
    )(pos, tab, mine, other, right, *stay(ours), *theirs)


def turn(core, buf, turned, some):
    for j in range(RING):
        at = slice(TILE * j, TILE * (j + 1))
        turned[at, :] = buf[:, at].T
        some[at, :] = buf[rows_at(2 * j + core, TILE), :]


def gram_first_body(pos, tab, mine, r0, r1, r2, r3, across, down, right, turned, some, sems):
    copies = []
    for k, ref in enumerate((r0, r1, r2, r3)):
        lanes = tile_at(lax.bitwise_xor(pos[0], k))
        copies.append(
            pltpu.make_async_copy(ref.at[BLOCK : 2 * BLOCK, :], right.at[:, lanes], sems.at[k])
        )
        copies[k].start()
    turn(pos[1], mine, turned, some)
    across[...] = dot(some[...], turned[...])
    down[...] = dot(turned[...], mine[...]).astype(BF16)
    for copy in copies:
        copy.wait()


def gram_first(pos, tab, mine, sides):
    return call(
        gram_first_body,
        (),
        [whole()] + [outside()] * RING,
        [whole()] * 3,
        [
            jax.ShapeDtypeStruct((HALF, BLOCK), F32),
            jax.ShapeDtypeStruct((HALF, HALF), BF16),
            jax.ShapeDtypeStruct((BLOCK, HALF), BF16),
        ],
        scratch=[
            pltpu.VMEM((HALF, BLOCK), BF16),
            pltpu.VMEM((HALF, HALF), BF16),
            pltpu.SemaphoreType.DMA((RING,)),
        ],
        flops=2 * BLOCK * BLOCK * HALF,
        moved=4 * BLOCK * BLOCK,
    )(pos, tab, mine, *stay(sides))


def gram_body(
    pos, tab, mine, other, half, down, step, step_other, o0, o1, o2, o3, turned, some, across, down_other, held, sems
):
    core = pos[1]
    outs = (o0, o1, o2, o3)
    copies = []

    def send(k, n, low, high):
        copy = pltpu.make_async_copy(
            held.at[k, low:high, :], outs[k].at[low:high, :], sems.at[k, n]
        )
        copy.start()
        copies.append(copy)

    turn(core, other, turned, some)
    across[...] = (half[...] + dot(some[...], turned[...])).astype(BF16)
    for k in range(RING):
        plane = lax.bitwise_xor(pos[0], k)
        for t in range(BLOCK // TILE):
            at = slice(TILE * t, TILE * (t + 1))
            held[k, at, :] = across[rows_at(plane, TILE), at]
        send(k, 0, 0, BLOCK)
    down_other[...] = dot(turned[...], mine[...]).astype(BF16)
    for k in range(RING):
        plane = lax.bitwise_xor(pos[0], k)
        for j in range(RING):
            at = slice(TILE * j, TILE * (j + 1))
            lanes = tile_at(plane)
            held[k, rows_at(BLOCK // TILE + 2 * j + core, TILE), :] = down[at, lanes]
            held[k, rows_at(BLOCK // TILE + 2 * j + 1 - core, TILE), :] = down_other[at, lanes]
        held[k, 2 * BLOCK : 2 * BLOCK + 16, :] = step[...]
        held[k, 2 * BLOCK + 16 : SHARE, :] = step_other[...]
        send(k, 1, BLOCK, SHARE)
    for copy in copies:
        copy.wait()


def gram(pos, tab, mine, other, half, down, step, step_other):
    return call(
        gram_body,
        (),
        [whole()] * 6,
        [outside()] * RING,
        [pltpu.HBM((SHARE, TILE), BF16)] * RING,
        scratch=[
            pltpu.VMEM((HALF, BLOCK), BF16),
            pltpu.VMEM((HALF, HALF), BF16),
            pltpu.VMEM((HALF, BLOCK), BF16),
            pltpu.VMEM((HALF, HALF), BF16),
            pltpu.VMEM((RING, SHARE, TILE), BF16),
            pltpu.SemaphoreType.DMA((RING, 2)),
        ],
        flops=2 * BLOCK * BLOCK * HALF,
        moved=8 * BLOCK * HALF,
    )(pos, tab, mine, other, half, down, step, step_other)


def stats_body(
    pos, tab, left, right, g0, g1, g2, g3, new_left, new_right, vec, rows, cols, held, sems, gram_sems
):
    gets = [pltpu.make_async_copy(g, held.at[k], gram_sems.at[k]) for k, g in enumerate((g0, g1, g2, g3))]
    loads, stores = [], []
    for s in range(SLOTS):
        pairs = ((left, rows, new_left), (right, cols, new_right))
        loads += [
            pltpu.make_async_copy(a.at[s], b.at[s], sems.at[0, s, n])
            for n, (a, b, c) in enumerate(pairs)
        ]
        stores += [
            pltpu.make_async_copy(b.at[s], c.at[s], sems.at[1, s, n])
            for n, (a, b, c) in enumerate(pairs)
        ]
    for copy in gets + loads:
        copy.start()
    for k in range(RING):
        gets[k].wait()
        plane = lax.bitwise_xor(pos[0], k)
        vec[:, tile_at(2 * plane + pos[1])] = held[k, 2 * BLOCK : 2 * BLOCK + 16, :]
        vec[:, tile_at(2 * plane + 1 - pos[1])] = held[k, 2 * BLOCK + 16 : SHARE, :]
    for s in range(SLOTS):
        source = tab[T_REL + s]
        some = source >= 0
        k = jnp.maximum(source, 0)
        loads[2 * s].wait()
        for t in range(BLOCK // TILE):
            at = slice(TILE * t, TILE * (t + 1))
            add = jnp.where(some, held[k, at, :].astype(F32), 0.0)
            rows[s, :, at] = BETA_STAT * rows[s, :, at] + (1.0 - BETA_STAT) * add
        stores[2 * s].start()
        loads[2 * s + 1].wait()
        add = jnp.where(some, held[k, BLOCK : 2 * BLOCK, :].astype(F32), 0.0)
        cols[s] = BETA_STAT * cols[s] + (1.0 - BETA_STAT) * add
        stores[2 * s + 1].start()
    for copy in stores:
        copy.wait()


def stats(pos, tab, left, right, grams):
    return call(
        stats_body,
        (),
        [outside()] * (2 + RING),
        [outside(), outside(), whole()],
        [
            jax.ShapeDtypeStruct((SLOTS, TILE, BLOCK), F32),
            jax.ShapeDtypeStruct((SLOTS, BLOCK, TILE), F32),
            jax.ShapeDtypeStruct((16, BLOCK), BF16),
        ],
        scratch=[
            pltpu.VMEM((SLOTS, TILE, BLOCK), F32),
            pltpu.VMEM((SLOTS, BLOCK, TILE), F32),
            pltpu.VMEM((RING, SHARE, TILE), BF16),
            pltpu.SemaphoreType.DMA((2, SLOTS, 2)),
            pltpu.SemaphoreType.DMA((RING,)),
        ],
        moved=16 * SLOTS * BLOCK * TILE + 16 * BLOCK * TILE,
    )(pos, tab, *stay([left, right, *grams]))


def back_body(pos, tab, got, out):
    for i in range(PER):
        at = rows_at(tab[T_OWNER + RING * i + pos[0]])
        out[ROWS * i : ROWS * (i + 1), :] = got[at, :]


def back(pos, tab, got):
    return call(
        back_body,
        (),
        [whole()],
        whole(),
        jax.ShapeDtypeStruct((BODY, HALF), BF16),
        moved=2 * (BLOCK + BODY) * HALF,
    )(pos, tab, got)


def place_body(parts, pos, tab, *refs):
    out, rows, sems = refs[-3:]
    core = pos[1]
    copies = []
    for n, (k, first, count) in enumerate(parts):
        plane = lax.bitwise_xor(pos[0], k)
        ours, theirs = refs[2 * n], refs[2 * n + 1]
        for i in range(count):
            at = slice(ROWS * i, ROWS * (i + 1))
            slab = len(copies)
            here = slice(ROWS * slab, ROWS * (slab + 1))
            for j in range(RING):
                lanes = slice(TILE * j, TILE * (j + 1))
                rows[here, tile_at(2 * j + core)] = ours[at, lanes]
                rows[here, tile_at(2 * j + 1 - core)] = theirs[at, lanes]
            target = out.at[rows_at(tab[RING * (first + i) + plane]), :]
            copies.append(pltpu.make_async_copy(rows.at[here, :], target, sems.at[slab]))
            copies[-1].start()
    for copy in copies:
        copy.wait()


def place(pos, tab, parts, arrays, onto=None):
    def place_part(*refs):
        place_body(parts, *refs)

    slabs = sum(count for _, _, count in parts)
    extra = () if onto is None else (onto,)
    return pl.pallas_call(
        place_part,
        name="place_part",
        grid_spec=pltpu.PrefetchScalarGridSpec(
            num_scalar_prefetch=2,
            grid=(),
            in_specs=[whole()] * (2 * len(parts)) + [outside()] * len(extra),
            out_specs=outside(),
            scratch_shapes=[
                pltpu.VMEM((ROWS * slabs, BLOCK), BF16),
                pltpu.SemaphoreType.DMA((slabs,)),
            ],
        ),
        out_shape=jax.ShapeDtypeStruct((FULL, BLOCK), BF16),
        input_output_aliases={} if onto is None else {2 + 2 * len(parts): 0},
        compiler_params=pltpu.CompilerParams(vmem_limit_bytes=VMEM_LIMIT),
        cost_estimate=pl.CostEstimate(
            flops=0, bytes_accessed=4 * ROWS * slabs * BLOCK, transcendentals=0
        ),
    )(pos, tab, *arrays, *extra)


def hop(x, k):
    return lax.ppermute(x, "y", [(i, i ^ k) for i in range(RING)])


def spread(x):
    far, near, other = lax.optimization_barrier((hop(x[2], 2), x[1], x[3]))
    return [x[0], hop(near, 1), far, hop(other, 3)]


def swap(x):
    return lax.ppermute(x, "core", [(0, 1), (1, 0)])


def route(x):
    x = x.reshape(OWNERS, ROWS, HALF)
    return lax.all_to_all(x, ("x", "z"), 0, 0).reshape(BLOCK, HALF)


def shards(
    grads,
    vec_grads,
    factor_left,
    factor_right,
    root_left,
    root_right,
    vec_param,
    vec_first,
    vec_second,
    bucket_block,
    block_slot,
    decay_mask,
):
    y, core = lax.axis_index("y"), lax.axis_index("core")
    owner = lax.axis_index(("x", "z"))
    pos = jnp.stack([y, core, owner]).astype(jnp.int32)
    grad = grads.reshape(FULL, BLOCK)
    got, got_vec = swap(grad), swap(vec_grads)
    tab, own = front(pos, jnp.concatenate([bucket_block, block_slot]), grad)
    give_a, keep_a, give_b, keep_b = pair(pos, tab, own, got, vec_grads, got_vec)
    got_a, got_b = hop(give_a, 1), hop(give_b, 3)
    last_a = hop(keep_a[A_ROWS:] + got_a[A_ROWS:], 3)
    last_b = hop(keep_b[BS_ROWS:] + got_b[BS_ROWS:], 1)
    parts = [keep_a, got_a, last_a, keep_b, got_b, last_b]
    sides = roots(pos, tab, root_left, root_right)
    parts, sides = lax.optimization_barrier((parts, sides))
    send, new_first, new_second, step = total(
        pos, tab, parts, vec_param, vec_first, vec_second, decay_mask
    )
    send, sides = lax.optimization_barrier((send, sides))
    sides = spread(sides)
    mine = route(send)
    step_other = swap(step)
    mine, sides, step_other = lax.optimization_barrier((mine, sides, step_other))
    other = swap(mine)
    across, down, right = gram_first(pos, tab, mine, sides)
    other, sides, across, down, right = lax.optimization_barrier(
        (other, sides, across, down, right)
    )
    grams = gram(pos, tab, mine, other, across, down, step, step_other)
    others = [swap(x) for x in sides]
    others, grams = lax.optimization_barrier((others, grams))
    result = update(pos, tab, mine, other, right, sides, others)
    result, grams = lax.optimization_barrier((result, grams))
    grams = spread(grams)
    got = route(result)
    got, *grams = lax.optimization_barrier((got, *grams))
    piece = back(pos, tab, got)
    near, near_other = hop(piece, 3), hop(piece, 1)
    new_left, new_right, vec_update = stats(pos, tab, factor_left, factor_right, grams)
    near, near_other, new_left, new_right, vec_update = lax.optimization_barrier(
        (near, near_other, new_left, new_right, vec_update[0:1])
    )
    far = [hop(near[:A_ROWS], 1), hop(near_other[A_ROWS:], 3)]
    both = []
    for x in (piece, near, near_other):
        both += [x, swap(x)]
    placed = place(pos, tab, ((0, 0, PER), (3, 0, PER), (1, 0, PER)), both)
    far, placed = lax.optimization_barrier((far, placed))
    both = [far[0], swap(far[0]), far[1], swap(far[1])]
    block_update = place(pos, tab, ((2, 0, HEAD), (2, HEAD, PER - HEAD)), both, placed)
    return (
        block_update.reshape(NBLK, ROWS, BLOCK),
        new_left,
        new_right,
        vec_update,
        new_first,
        new_second,
    )


def solution(mesh):
    fine = Mesh(mesh.devices.reshape(RING, CORES, 4, 8), ("y", "core", "x", "z"))
    dp, shard = ("y", "core"), ("x", "z")
    return jax.shard_map(
        shards,
        mesh=fine,
        in_specs=(
            P(dp, None, shard, None),
            P(dp, shard, None),
            P(shard, dp, None),
            P(shard, None, dp),
            P(shard, None, dp),
            P(shard, None, dp),
            P(shard, dp),
            P(shard, dp),
            P(shard, dp),
            P(),
            P(),
            P(shard, dp),
        ),
        out_specs=(
            P(None, shard, None),
            P(shard, dp, None),
            P(shard, None, dp),
            P(shard, None),
            P(shard, dp),
            P(shard, dp),
        ),
        check_vma=False,
    )
```

```python
import jax
import jax.numpy as jnp
from jax import lax
from jax.experimental import pallas as pl
from jax.experimental.pallas import tpu as pltpu
from jax.sharding import Mesh
from jax.sharding import PartitionSpec as P

BETA_STAT = 0.95
ADAM_ONE = 0.9
ADAM_TWO = 0.95
ADAM_EPS = 1e-08
DECAY = 0.1

RING = 4
CORES = 2
OWNERS = 32
SLOTS = 3
NBLK = 36
PER = NBLK // RING
BLOCK = 1024
ROWS = BLOCK // OWNERS
TILE = 128
PASS = 512
HALF = BLOCK // CORES
BODY = PER * ROWS
HEAD = (PER + 1) // 2
A_ROWS = HEAD * ROWS
B_ROWS = BODY - A_ROWS
BS_ROWS = B_ROWS + 16
SHARE = 2 * BLOCK + 32
FULL = NBLK * ROWS
BF16 = jnp.bfloat16
F32 = jnp.float32
T_OWNER = 40
T_SEL = 80
T_REL = 84
TABLE = 88
VMEM_LIMIT = 24 * 1024 * 1024


def whole():
    return pl.BlockSpec(memory_space=pltpu.VMEM)


def call(
    body, grid, in_specs, out_specs, out_shape, scratch=(), flops=0, moved=0, limit=VMEM_LIMIT
):
    return pl.pallas_call(
        body,
        name=body.__name__,
        grid_spec=pltpu.PrefetchScalarGridSpec(
            num_scalar_prefetch=2,
            grid=grid,
            in_specs=in_specs,
            out_specs=out_specs,
            scratch_shapes=list(scratch),
        ),
        out_shape=out_shape,
        compiler_params=pltpu.CompilerParams(vmem_limit_bytes=limit),
        cost_estimate=pl.CostEstimate(flops=flops, bytes_accessed=moved, transcendentals=0),
    )


def outside():
    return pl.BlockSpec(memory_space=pltpu.HBM)


def stay(x):
    return jax.tree.map(lambda a: pltpu.with_memory_space_constraint(a, pltpu.HBM), x)


def tile_at(index):
    return pl.ds(pl.multiple_of(index * TILE, TILE), TILE)


def rows_at(index, size=ROWS):
    return pl.ds(pl.multiple_of(index * size, size), size)


def dot(a, b):
    return jnp.dot(a, b, preferred_element_type=F32)


def front_body(pos, spare, maps, grad, vec, tab, own, own_vec, seat, ranks, sems):
    copies = [
        pltpu.make_async_copy(grad.at[:, tile_at(2 * j + pos[1])], own.at[j], sems.at[j])
        for j in range(RING)
    ]
    copies.append(pltpu.make_async_copy(vec, own_vec, sems.at[RING]))
    for copy in copies:
        copy.start()
    for s in range(OWNERS * SLOTS):
        seat[s] = -1
    for p in range(NBLK):
        seat[maps[NBLK + maps[p]]] = p
    for k in range(RING):
        tab[T_SEL + k] = 0
    rank = jnp.int32(0)
    for s in range(OWNERS * SLOTS):
        p = seat[s]
        tab[rank] = p
        tab[T_OWNER + rank] = s // SLOTS
        ranks[s] = rank
        rank = rank + jnp.where(p >= 0, 1, 0)
    for k in range(SLOTS):
        s = pos[2] * SLOTS + k
        held = seat[s] >= 0
        plane = lax.rem(ranks[s], RING)
        tab[T_REL + k] = jnp.where(held, lax.bitwise_xor(pos[0], plane), -1)
        ahead = T_SEL + lax.bitwise_xor(pos[0], plane)
        tab[ahead] = jnp.where(held, k, tab[ahead])
    for copy in copies:
        copy.wait()


def front(pos, maps, grad, vec):
    smem = pl.BlockSpec(memory_space=pltpu.SMEM)
    return call(
        front_body,
        (),
        [smem, outside(), outside()],
        [smem, whole(), whole()],
        [
            jax.ShapeDtypeStruct((TABLE,), jnp.int32),
            jax.ShapeDtypeStruct((RING, FULL, TILE), BF16),
            jax.ShapeDtypeStruct((1, 1, BLOCK), BF16),
        ],
        scratch=[
            pltpu.SMEM((OWNERS * SLOTS,), jnp.int32),
            pltpu.SMEM((OWNERS * SLOTS,), jnp.int32),
            pltpu.SemaphoreType.DMA((RING + 1,)),
        ],
        moved=4 * FULL * HALF,
    )(pos, pos, maps, stay(grad), stay(vec))


def pair_body(pos, tab, own, got, vec, got_vec, give_a, keep_a, give_b, keep_b):
    lanes_of = [tile_at(2 * j + pos[1]) for j in range(RING)]
    first = {0: (keep_a, 0), 3: (keep_a, 1), 1: (give_a, 0), 2: (give_a, 1)}
    second = {0: (keep_b, 0), 1: (keep_b, 1), 3: (give_b, 0), 2: (give_b, 1)}
    for k in range(RING):
        plane = lax.bitwise_xor(pos[0], k)
        for i in range(PER):
            at = rows_at(tab[RING * i + plane])
            out, part = first[k] if i < HEAD else second[k]
            low = part * A_ROWS + ROWS * i if i < HEAD else part * BS_ROWS + ROWS * (i - HEAD)
            for j, lanes in enumerate(lanes_of):
                here = slice(TILE * j, TILE * (j + 1))
                out[low : low + ROWS, here] = own[j, at, :] + got[at, lanes]
    for j, lanes in enumerate(lanes_of):
        both = vec[0, :, lanes].astype(F32) + got_vec[0, :, lanes].astype(F32)
        strip = jnp.broadcast_to(both, (16, TILE)).astype(BF16)
        for out, part in second.values():
            low = part * BS_ROWS + B_ROWS
            out[low : low + 16, TILE * j : TILE * (j + 1)] = strip


def pair(pos, tab, own, got, vec, got_vec):
    return call(
        pair_body,
        (),
        [whole()] * 4,
        [whole()] * 4,
        [jax.ShapeDtypeStruct((2 * n, HALF), BF16) for n in (A_ROWS, A_ROWS, BS_ROWS, BS_ROWS)],
        moved=6 * FULL * HALF,
    )(pos, tab, own, got, vec, got_vec)


def total_body(
    pos, tab, a0, a1, a2, b0, b1, b2, param, first, second, mask, send, new_first, new_second, step
):
    send[...] = jnp.zeros(send.shape, BF16)
    for i in range(PER):
        refs, low = ((a0, a1, a2), ROWS * i) if i < HEAD else ((b0, b1, b2), ROWS * (i - HEAD))
        parts = [ref[low : low + ROWS, :].astype(F32) for ref in refs]
        total = (parts[0] + parts[1]) + parts[2]
        send[rows_at(tab[T_OWNER + RING * i + pos[0]]), :] = total.astype(BF16)
    strips = [ref[B_ROWS:BS_ROWS, tile_at(pos[0])].astype(F32) for ref in (b0, b1, b2)]
    vec_sum = ((strips[0] + strips[1]) + strips[2])[0:1]
    one = ADAM_ONE * first[...] + (1.0 - ADAM_ONE) * vec_sum
    two = ADAM_TWO * second[...] + (1.0 - ADAM_TWO) * vec_sum * vec_sum
    new_first[...] = one
    new_second[...] = two
    update = one / (jnp.sqrt(two) + ADAM_EPS) + DECAY * mask[...].astype(F32) * param[...]
    step[...] = jnp.broadcast_to(update, (16, TILE)).astype(BF16)


def total(pos, tab, parts, param, first, second, mask):
    return call(
        total_body,
        (),
        [whole()] * 10,
        [whole()] * 4,
        [
            pltpu.HBM((BLOCK, HALF), BF16),
            jax.ShapeDtypeStruct((1, TILE), F32),
            jax.ShapeDtypeStruct((1, TILE), F32),
            jax.ShapeDtypeStruct((16, TILE), BF16),
        ],
        moved=12 * BODY * HALF + 2 * BLOCK * HALF,
    )(pos, tab, *parts, param, first, second, mask)


def roots_body(pos, tab, left, right, *outs):
    for k in range(RING):
        slot = tab[T_SEL + k]
        outs[k][0:BLOCK, :] = left[slot]
        for j in range(RING):
            for n, tile in enumerate((2 * j + pos[1], 2 * j + 1 - pos[1])):
                at = BLOCK + HALF * n + TILE * j
                outs[k][at : at + TILE, :] = right[slot, rows_at(tile, TILE), :]


def roots(pos, tab, left, right):
    return call(
        roots_body,
        (),
        [whole()] * 2,
        [whole()] * RING,
        [pltpu.HBM((2 * BLOCK, TILE), BF16)] * RING,
        moved=4 * (SLOTS + RING) * BLOCK * TILE,
    )(pos, tab, left, right)


def update_body(pos, tab, mine, other, right, *refs):
    ours, theirs = refs[:RING], refs[RING : 2 * RING]
    out, left, applied, result, sems, out_sems = refs[2 * RING :]
    core = pos[1]
    copies = []
    for k in range(RING):
        plane = lax.bitwise_xor(pos[0], k)
        for n, (ref, tile) in enumerate(((ours[k], 2 * plane + core), (theirs[k], 2 * plane + 1 - core))):
            copies.append(
                pltpu.make_async_copy(ref.at[0:BLOCK, :], left.at[:, tile_at(tile)], sems.at[n, k])
            )
    for copy in copies:
        copy.start()
    applied[...] = (
        dot(mine[...], right[0:HALF, :]) + dot(other[...], right[HALF:BLOCK, :])
    ).astype(BF16)
    for copy in copies:
        copy.wait()
    stores = []
    for n in range(BLOCK // PASS):
        at = slice(PASS * n, PASS * (n + 1))
        result[at, :] = dot(left[at, :], applied[...]).astype(BF16)
        stores.append(pltpu.make_async_copy(result.at[at, :], out.at[at, :], out_sems.at[n]))
        stores[n].start()
    for copy in stores:
        copy.wait()


def update(pos, tab, mine, other, right, ours, theirs):
    return call(
        update_body,
        (),
        [whole()] * 3 + [outside()] * (2 * RING),
        outside(),
        pltpu.HBM((BLOCK, HALF), BF16),
        scratch=[
            pltpu.VMEM((BLOCK, BLOCK), BF16),
            pltpu.VMEM((BLOCK, HALF), BF16),
            pltpu.VMEM((BLOCK, HALF), BF16),
            pltpu.SemaphoreType.DMA((2, RING)),
            pltpu.SemaphoreType.DMA((BLOCK // PASS,)),
        ],
        flops=4 * BLOCK * BLOCK * HALF,
        moved=16 * BLOCK * HALF,
    )(pos, tab, mine, other, right, *stay(ours), *theirs)


def turn(core, buf, turned, some):
    for j in range(RING):
        at = slice(TILE * j, TILE * (j + 1))
        turned[at, :] = buf[:, at].T
        some[at, :] = buf[rows_at(2 * j + core, TILE), :]


def gram_first_body(pos, tab, mine, r0, r1, r2, r3, across, down, right, turned, some, sems):
    copies = []
    for k, ref in enumerate((r0, r1, r2, r3)):
        lanes = tile_at(lax.bitwise_xor(pos[0], k))
        copies.append(
            pltpu.make_async_copy(ref.at[BLOCK : 2 * BLOCK, :], right.at[:, lanes], sems.at[k])
        )
        copies[k].start()
    turn(pos[1], mine, turned, some)
    across[...] = dot(some[...], turned[...])
    down[...] = dot(turned[...], mine[...]).astype(BF16)
    for copy in copies:
        copy.wait()


def gram_first(pos, tab, mine, sides):
    return call(
        gram_first_body,
        (),
        [whole()] + [outside()] * RING,
        [whole()] * 3,
        [
            jax.ShapeDtypeStruct((HALF, BLOCK), F32),
            jax.ShapeDtypeStruct((HALF, HALF), BF16),
            jax.ShapeDtypeStruct((BLOCK, HALF), BF16),
        ],
        scratch=[
            pltpu.VMEM((HALF, BLOCK), BF16),
            pltpu.VMEM((HALF, HALF), BF16),
            pltpu.SemaphoreType.DMA((RING,)),
        ],
        flops=2 * BLOCK * BLOCK * HALF,
        moved=4 * BLOCK * BLOCK,
    )(pos, tab, mine, *stay(sides))


def gram_body(
    pos, tab, mine, other, half, down, step, step_other, o0, o1, o2, o3, turned, some, across, down_other, held, sems
):
    core = pos[1]
    outs = (o0, o1, o2, o3)
    copies = []

    def send(k, n, low, high):
        copy = pltpu.make_async_copy(
            held.at[k, low:high, :], outs[k].at[low:high, :], sems.at[k, n]
        )
        copy.start()
        copies.append(copy)

    turn(core, other, turned, some)
    across[...] = (half[...] + dot(some[...], turned[...])).astype(BF16)
    for k in range(RING):
        plane = lax.bitwise_xor(pos[0], k)
        for t in range(BLOCK // TILE):
            at = slice(TILE * t, TILE * (t + 1))
            held[k, at, :] = across[rows_at(plane, TILE), at]
        send(k, 0, 0, BLOCK)
    down_other[...] = dot(turned[...], mine[...]).astype(BF16)
    for k in range(RING):
        plane = lax.bitwise_xor(pos[0], k)
        for j in range(RING):
            at = slice(TILE * j, TILE * (j + 1))
            lanes = tile_at(plane)
            held[k, rows_at(BLOCK // TILE + 2 * j + core, TILE), :] = down[at, lanes]
            held[k, rows_at(BLOCK // TILE + 2 * j + 1 - core, TILE), :] = down_other[at, lanes]
        held[k, 2 * BLOCK : 2 * BLOCK + 16, :] = step[...]
        held[k, 2 * BLOCK + 16 : SHARE, :] = step_other[...]
        send(k, 1, BLOCK, SHARE)
    for copy in copies:
        copy.wait()


def gram(pos, tab, mine, other, half, down, step, step_other):
    return call(
        gram_body,
        (),
        [whole()] * 6,
        [outside()] * RING,
        [pltpu.HBM((SHARE, TILE), BF16)] * RING,
        scratch=[
            pltpu.VMEM((HALF, BLOCK), BF16),
            pltpu.VMEM((HALF, HALF), BF16),
            pltpu.VMEM((HALF, BLOCK), BF16),
            pltpu.VMEM((HALF, HALF), BF16),
            pltpu.VMEM((RING, SHARE, TILE), BF16),
            pltpu.SemaphoreType.DMA((RING, 2)),
        ],
        flops=2 * BLOCK * BLOCK * HALF,
        moved=8 * BLOCK * HALF,
    )(pos, tab, mine, other, half, down, step, step_other)


def stats_body(
    pos, tab, left, right, g0, g1, g2, g3, new_left, new_right, vec, rows, cols, held, sems, gram_sems
):
    gets = [pltpu.make_async_copy(g, held.at[k], gram_sems.at[k]) for k, g in enumerate((g0, g1, g2, g3))]
    loads, stores = [], []
    for s in range(SLOTS):
        pairs = ((left, rows, new_left), (right, cols, new_right))
        loads += [
            pltpu.make_async_copy(a.at[s], b.at[s], sems.at[0, s, n])
            for n, (a, b, c) in enumerate(pairs)
        ]
        stores += [
            pltpu.make_async_copy(b.at[s], c.at[s], sems.at[1, s, n])
            for n, (a, b, c) in enumerate(pairs)
        ]
    for copy in gets + loads:
        copy.start()
    for k in range(RING):
        gets[k].wait()
        plane = lax.bitwise_xor(pos[0], k)
        vec[:, tile_at(2 * plane + pos[1])] = held[k, 2 * BLOCK : 2 * BLOCK + 16, :]
        vec[:, tile_at(2 * plane + 1 - pos[1])] = held[k, 2 * BLOCK + 16 : SHARE, :]
    for s in range(SLOTS):
        source = tab[T_REL + s]
        some = source >= 0
        k = jnp.maximum(source, 0)
        loads[2 * s].wait()
        for t in range(BLOCK // TILE):
            at = slice(TILE * t, TILE * (t + 1))
            add = jnp.where(some, held[k, at, :].astype(F32), 0.0)
            rows[s, :, at] = BETA_STAT * rows[s, :, at] + (1.0 - BETA_STAT) * add
        stores[2 * s].start()
        loads[2 * s + 1].wait()
        add = jnp.where(some, held[k, BLOCK : 2 * BLOCK, :].astype(F32), 0.0)
        cols[s] = BETA_STAT * cols[s] + (1.0 - BETA_STAT) * add
        stores[2 * s + 1].start()
    for copy in stores:
        copy.wait()


def stats(pos, tab, left, right, grams):
    return call(
        stats_body,
        (),
        [outside()] * (2 + RING),
        [outside(), outside(), whole()],
        [
            jax.ShapeDtypeStruct((SLOTS, TILE, BLOCK), F32),
            jax.ShapeDtypeStruct((SLOTS, BLOCK, TILE), F32),
            jax.ShapeDtypeStruct((16, BLOCK), BF16),
        ],
        scratch=[
            pltpu.VMEM((SLOTS, TILE, BLOCK), F32),
            pltpu.VMEM((SLOTS, BLOCK, TILE), F32),
            pltpu.VMEM((RING, SHARE, TILE), BF16),
            pltpu.SemaphoreType.DMA((2, SLOTS, 2)),
            pltpu.SemaphoreType.DMA((RING,)),
        ],
        moved=16 * SLOTS * BLOCK * TILE + 16 * BLOCK * TILE,
    )(pos, tab, *stay([left, right, *grams]))


def back_body(pos, tab, got, out):
    for i in range(PER):
        at = rows_at(tab[T_OWNER + RING * i + pos[0]])
        out[ROWS * i : ROWS * (i + 1), :] = got[at, :]


def back(pos, tab, got):
    return call(
        back_body,
        (),
        [whole()],
        whole(),
        jax.ShapeDtypeStruct((BODY, HALF), BF16),
        moved=2 * (BLOCK + BODY) * HALF,
    )(pos, tab, got)


def place_body(parts, pos, tab, *refs):
    out, rows, sems = refs[-3:]
    core = pos[1]
    copies = []
    for n, (k, first, count) in enumerate(parts):
        plane = lax.bitwise_xor(pos[0], k)
        ours, theirs = refs[2 * n], refs[2 * n + 1]
        for i in range(count):
            at = slice(ROWS * i, ROWS * (i + 1))
            slab = len(copies)
            here = slice(ROWS * slab, ROWS * (slab + 1))
            for j in range(RING):
                lanes = slice(TILE * j, TILE * (j + 1))
                rows[here, tile_at(2 * j + core)] = ours[at, lanes]
                rows[here, tile_at(2 * j + 1 - core)] = theirs[at, lanes]
            target = out.at[rows_at(tab[RING * (first + i) + plane]), :]
            copies.append(pltpu.make_async_copy(rows.at[here, :], target, sems.at[slab]))
            copies[-1].start()
    for copy in copies:
        copy.wait()


def place(pos, tab, parts, arrays, onto=None):
    def place_part(*refs):
        place_body(parts, *refs)

    slabs = sum(count for _, _, count in parts)
    extra = () if onto is None else (onto,)
    return pl.pallas_call(
        place_part,
        name="place_part",
        grid_spec=pltpu.PrefetchScalarGridSpec(
            num_scalar_prefetch=2,
            grid=(),
            in_specs=[whole()] * (2 * len(parts)) + [outside()] * len(extra),
            out_specs=outside(),
            scratch_shapes=[
                pltpu.VMEM((ROWS * slabs, BLOCK), BF16),
                pltpu.SemaphoreType.DMA((slabs,)),
            ],
        ),
        out_shape=jax.ShapeDtypeStruct((FULL, BLOCK), BF16),
        input_output_aliases={} if onto is None else {2 + 2 * len(parts): 0},
        compiler_params=pltpu.CompilerParams(vmem_limit_bytes=VMEM_LIMIT),
        cost_estimate=pl.CostEstimate(
            flops=0, bytes_accessed=4 * ROWS * slabs * BLOCK, transcendentals=0
        ),
    )(pos, tab, *arrays, *extra)


def hop(x, k):
    return lax.ppermute(x, "y", [(i, i ^ k) for i in range(RING)])


def spread(x):
    far, near, other = lax.optimization_barrier((hop(x[2], 2), x[1], x[3]))
    return [x[0], hop(near, 1), far, hop(other, 3)]


def swap(x):
    return lax.ppermute(x, "core", [(0, 1), (1, 0)])


def route(x):
    x = x.reshape(OWNERS, ROWS, HALF)
    return lax.all_to_all(x, ("x", "z"), 0, 0).reshape(BLOCK, HALF)


def shards(
    grads,
    vec_grads,
    factor_left,
    factor_right,
    root_left,
    root_right,
    vec_param,
    vec_first,
    vec_second,
    bucket_block,
    block_slot,
    decay_mask,
):
    y, core = lax.axis_index("y"), lax.axis_index("core")
    owner = lax.axis_index(("x", "z"))
    pos = jnp.stack([y, core, owner]).astype(jnp.int32)
    grad = grads.reshape(FULL, BLOCK)
    got, got_vec = swap(grad), swap(vec_grads)
    tab, own, vec = front(pos, jnp.concatenate([bucket_block, block_slot]), grad, vec_grads)
    give_a, keep_a, give_b, keep_b = pair(pos, tab, own, got, vec, got_vec)
    got_a, got_b = hop(give_a, 1), hop(give_b, 3)
    last_a = hop(keep_a[A_ROWS:] + got_a[A_ROWS:], 3)
    last_b = hop(keep_b[BS_ROWS:] + got_b[BS_ROWS:], 1)
    parts = [keep_a, got_a, last_a, keep_b, got_b, last_b]
    sides = roots(pos, tab, root_left, root_right)
    parts, sides = lax.optimization_barrier((parts, sides))
    send, new_first, new_second, step = total(
        pos, tab, parts, vec_param, vec_first, vec_second, decay_mask
    )
    send, sides = lax.optimization_barrier((send, sides))
    sides = spread(sides)
    mine = route(send)
    step_other = swap(step)
    mine, sides, step_other = lax.optimization_barrier((mine, sides, step_other))
    other = swap(mine)
    across, down, right = gram_first(pos, tab, mine, sides)
    other, sides, across, down, right = lax.optimization_barrier(
        (other, sides, across, down, right)
    )
    grams = gram(pos, tab, mine, other, across, down, step, step_other)
    others = [swap(x) for x in sides]
    others, grams = lax.optimization_barrier((others, grams))
    result = update(pos, tab, mine, other, right, sides, others)
    result, grams = lax.optimization_barrier((result, grams))
    near, other_near, far = hop(grams[1], 1), hop(grams[3], 3), hop(grams[2], 2)
    got = route(result)
    got, near, other_near, far = lax.optimization_barrier((got, near, other_near, far))
    grams = [grams[0], near, far, other_near]
    piece = back(pos, tab, got)
    near, near_other = hop(piece, 3), hop(piece, 1)
    new_left, new_right, vec_update = stats(pos, tab, factor_left, factor_right, grams)
    near, near_other, new_left, new_right, vec_update = lax.optimization_barrier(
        (near, near_other, new_left, new_right, vec_update[0:1])
    )
    far = [hop(near[:A_ROWS], 1), hop(near_other[A_ROWS:], 3)]
    both = []
    for x in (piece, near, near_other):
        both += [x, swap(x)]
    placed = place(pos, tab, ((0, 0, PER), (3, 0, PER), (1, 0, PER)), both)
    far, placed = lax.optimization_barrier((far, placed))
    both = [far[0], swap(far[0]), far[1], swap(far[1])]
    block_update = place(pos, tab, ((2, 0, HEAD), (2, HEAD, PER - HEAD)), both, placed)
    return (
        block_update.reshape(NBLK, ROWS, BLOCK),
        new_left,
        new_right,
        vec_update,
        new_first,
        new_second,
    )


def solution(mesh):
    fine = Mesh(mesh.devices.reshape(RING, CORES, 4, 8), ("y", "core", "x", "z"))
    dp, shard = ("y", "core"), ("x", "z")
    return jax.shard_map(
        shards,
        mesh=fine,
        in_specs=(
            P(dp, None, shard, None),
            P(dp, shard, None),
            P(shard, dp, None),
            P(shard, None, dp),
            P(shard, None, dp),
            P(shard, None, dp),
            P(shard, dp),
            P(shard, dp),
            P(shard, dp),
            P(),
            P(),
            P(shard, dp),
        ),
        out_specs=(
            P(None, shard, None),
            P(shard, dp, None),
            P(shard, None, dp),
            P(shard, None),
            P(shard, dp),
            P(shard, dp),
        ),
        check_vma=False,
    )
```

```python
import jax
import jax.numpy as jnp
from jax import lax
from jax.experimental import pallas as pl
from jax.experimental.pallas import tpu as pltpu
from jax.sharding import Mesh
from jax.sharding import PartitionSpec as P

BETA_STAT = 0.95
ADAM_ONE = 0.9
ADAM_TWO = 0.95
ADAM_EPS = 1e-08
DECAY = 0.1

RING = 4
CORES = 2
OWNERS = 32
SLOTS = 3
NBLK = 36
PER = NBLK // RING
BLOCK = 1024
ROWS = BLOCK // OWNERS
TILE = 128
PASS = 512
HALF = BLOCK // CORES
BODY = PER * ROWS
HEAD = (PER + 1) // 2
A_ROWS = HEAD * ROWS
B_ROWS = BODY - A_ROWS
BS_ROWS = B_ROWS + 16
SHARE = 2 * BLOCK + 32
FULL = NBLK * ROWS
BF16 = jnp.bfloat16
F32 = jnp.float32
T_OWNER = 40
T_SEL = 80
T_REL = 84
TABLE = 88
VMEM_LIMIT = 24 * 1024 * 1024


def whole():
    return pl.BlockSpec(memory_space=pltpu.VMEM)


def call(
    body, grid, in_specs, out_specs, out_shape, scratch=(), flops=0, moved=0, limit=VMEM_LIMIT
):
    return pl.pallas_call(
        body,
        name=body.__name__,
        grid_spec=pltpu.PrefetchScalarGridSpec(
            num_scalar_prefetch=2,
            grid=grid,
            in_specs=in_specs,
            out_specs=out_specs,
            scratch_shapes=list(scratch),
        ),
        out_shape=out_shape,
        compiler_params=pltpu.CompilerParams(vmem_limit_bytes=limit),
        cost_estimate=pl.CostEstimate(flops=flops, bytes_accessed=moved, transcendentals=0),
    )


def outside():
    return pl.BlockSpec(memory_space=pltpu.HBM)


def stay(x):
    return jax.tree.map(lambda a: pltpu.with_memory_space_constraint(a, pltpu.HBM), x)


def tile_at(index):
    return pl.ds(pl.multiple_of(index * TILE, TILE), TILE)


def rows_at(index, size=ROWS):
    return pl.ds(pl.multiple_of(index * size, size), size)


def dot(a, b):
    return jnp.dot(a, b, preferred_element_type=F32)


def front_body(pos, spare, maps, grad, vec, tab, own, own_vec, seat, ranks, sems):
    copies = [
        pltpu.make_async_copy(grad.at[:, tile_at(2 * j + pos[1])], own.at[j], sems.at[j])
        for j in range(RING)
    ]
    copies.append(pltpu.make_async_copy(vec, own_vec, sems.at[RING]))
    for copy in copies:
        copy.start()
    for s in range(OWNERS * SLOTS):
        seat[s] = -1
    for p in range(NBLK):
        seat[maps[NBLK + maps[p]]] = p
    for k in range(RING):
        tab[T_SEL + k] = 0
    rank = jnp.int32(0)
    for s in range(OWNERS * SLOTS):
        p = seat[s]
        tab[rank] = p
        tab[T_OWNER + rank] = s // SLOTS
        ranks[s] = rank
        rank = rank + jnp.where(p >= 0, 1, 0)
    for k in range(SLOTS):
        s = pos[2] * SLOTS + k
        held = seat[s] >= 0
        plane = lax.rem(ranks[s], RING)
        tab[T_REL + k] = jnp.where(held, lax.bitwise_xor(pos[0], plane), -1)
        ahead = T_SEL + lax.bitwise_xor(pos[0], plane)
        tab[ahead] = jnp.where(held, k, tab[ahead])
    for copy in copies:
        copy.wait()


def front(pos, maps, grad, vec):
    smem = pl.BlockSpec(memory_space=pltpu.SMEM)
    return call(
        front_body,
        (),
        [smem, outside(), outside()],
        [smem, whole(), whole()],
        [
            jax.ShapeDtypeStruct((TABLE,), jnp.int32),
            jax.ShapeDtypeStruct((RING, FULL, TILE), BF16),
            jax.ShapeDtypeStruct((1, 1, BLOCK), BF16),
        ],
        scratch=[
            pltpu.SMEM((OWNERS * SLOTS,), jnp.int32),
            pltpu.SMEM((OWNERS * SLOTS,), jnp.int32),
            pltpu.SemaphoreType.DMA((RING + 1,)),
        ],
        moved=4 * FULL * HALF,
    )(pos, pos, maps, stay(grad), stay(vec))


def pair_body(pos, tab, own, got, vec, got_vec, give_a, keep_a, give_b, keep_b):
    lanes_of = [tile_at(2 * j + pos[1]) for j in range(RING)]
    first = {0: (keep_a, 0), 3: (keep_a, 1), 1: (give_a, 0), 2: (give_a, 1)}
    second = {0: (keep_b, 0), 1: (keep_b, 1), 3: (give_b, 0), 2: (give_b, 1)}
    for k in range(RING):
        plane = lax.bitwise_xor(pos[0], k)
        for i in range(PER):
            at = rows_at(tab[RING * i + plane])
            out, part = first[k] if i < HEAD else second[k]
            low = part * A_ROWS + ROWS * i if i < HEAD else part * BS_ROWS + ROWS * (i - HEAD)
            for j, lanes in enumerate(lanes_of):
                here = slice(TILE * j, TILE * (j + 1))
                out[low : low + ROWS, here] = own[j, at, :] + got[at, lanes]
    for j, lanes in enumerate(lanes_of):
        both = vec[0, :, lanes].astype(F32) + got_vec[0, :, lanes].astype(F32)
        strip = jnp.broadcast_to(both, (16, TILE)).astype(BF16)
        for out, part in second.values():
            low = part * BS_ROWS + B_ROWS
            out[low : low + 16, TILE * j : TILE * (j + 1)] = strip


def pair(pos, tab, own, got, vec, got_vec):
    return call(
        pair_body,
        (),
        [whole()] * 4,
        [whole()] * 4,
        [jax.ShapeDtypeStruct((2 * n, HALF), BF16) for n in (A_ROWS, A_ROWS, BS_ROWS, BS_ROWS)],
        moved=6 * FULL * HALF,
    )(pos, tab, own, got, vec, got_vec)


def total_body(
    pos, tab, a0, a1, a2, b0, b1, b2, param, first, second, mask, send, new_first, new_second, step
):
    send[...] = jnp.zeros(send.shape, BF16)
    for i in range(PER):
        refs, low = ((a0, a1, a2), ROWS * i) if i < HEAD else ((b0, b1, b2), ROWS * (i - HEAD))
        parts = [ref[low : low + ROWS, :].astype(F32) for ref in refs]
        total = (parts[0] + parts[1]) + parts[2]
        send[rows_at(tab[T_OWNER + RING * i + pos[0]]), :] = total.astype(BF16)
    strips = [ref[B_ROWS:BS_ROWS, tile_at(pos[0])].astype(F32) for ref in (b0, b1, b2)]
    vec_sum = ((strips[0] + strips[1]) + strips[2])[0:1]
    one = ADAM_ONE * first[...] + (1.0 - ADAM_ONE) * vec_sum
    two = ADAM_TWO * second[...] + (1.0 - ADAM_TWO) * vec_sum * vec_sum
    new_first[...] = one
    new_second[...] = two
    update = one / (jnp.sqrt(two) + ADAM_EPS) + DECAY * mask[...].astype(F32) * param[...]
    step[...] = jnp.broadcast_to(update, (16, TILE)).astype(BF16)


def total(pos, tab, parts, param, first, second, mask):
    return call(
        total_body,
        (),
        [whole()] * 10,
        [whole()] * 4,
        [
            pltpu.HBM((BLOCK, HALF), BF16),
            jax.ShapeDtypeStruct((1, TILE), F32),
            jax.ShapeDtypeStruct((1, TILE), F32),
            jax.ShapeDtypeStruct((16, TILE), BF16),
        ],
        moved=12 * BODY * HALF + 2 * BLOCK * HALF,
    )(pos, tab, *parts, param, first, second, mask)


def roots_body(pos, tab, left, right, *outs):
    for k in range(RING):
        slot = tab[T_SEL + k]
        outs[k][0:BLOCK, :] = left[slot]
        for j in range(RING):
            for n, tile in enumerate((2 * j + pos[1], 2 * j + 1 - pos[1])):
                at = BLOCK + HALF * n + TILE * j
                outs[k][at : at + TILE, :] = right[slot, rows_at(tile, TILE), :]


def roots(pos, tab, left, right):
    return call(
        roots_body,
        (),
        [whole()] * 2,
        [whole()] * RING,
        [pltpu.HBM((2 * BLOCK, TILE), BF16)] * RING,
        moved=4 * (SLOTS + RING) * BLOCK * TILE,
    )(pos, tab, left, right)


def update_body(pos, tab, mine, other, right, *refs):
    ours, theirs = refs[:RING], refs[RING : 2 * RING]
    out, left, applied, result, sems, out_sems = refs[2 * RING :]
    core = pos[1]
    copies = []
    for k in range(RING):
        plane = lax.bitwise_xor(pos[0], k)
        for n, (ref, tile) in enumerate(((ours[k], 2 * plane + core), (theirs[k], 2 * plane + 1 - core))):
            copies.append(
                pltpu.make_async_copy(ref.at[0:BLOCK, :], left.at[:, tile_at(tile)], sems.at[n, k])
            )
    for copy in copies:
        copy.start()
    applied[...] = (
        dot(mine[...], right[0:HALF, :]) + dot(other[...], right[HALF:BLOCK, :])
    ).astype(BF16)
    for copy in copies:
        copy.wait()
    stores = []
    for n in range(BLOCK // PASS):
        at = slice(PASS * n, PASS * (n + 1))
        result[at, :] = dot(left[at, :], applied[...]).astype(BF16)
        stores.append(pltpu.make_async_copy(result.at[at, :], out.at[at, :], out_sems.at[n]))
        stores[n].start()
    for copy in stores:
        copy.wait()


def update(pos, tab, mine, other, right, ours, theirs):
    return call(
        update_body,
        (),
        [whole()] * 3 + [outside()] * (2 * RING),
        outside(),
        pltpu.HBM((BLOCK, HALF), BF16),
        scratch=[
            pltpu.VMEM((BLOCK, BLOCK), BF16),
            pltpu.VMEM((BLOCK, HALF), BF16),
            pltpu.VMEM((BLOCK, HALF), BF16),
            pltpu.SemaphoreType.DMA((2, RING)),
            pltpu.SemaphoreType.DMA((BLOCK // PASS,)),
        ],
        flops=4 * BLOCK * BLOCK * HALF,
        moved=16 * BLOCK * HALF,
    )(pos, tab, mine, other, right, *stay(ours), *theirs)


def turn(core, buf, turned, some):
    for j in range(RING):
        at = slice(TILE * j, TILE * (j + 1))
        turned[at, :] = buf[:, at].T
        some[at, :] = buf[rows_at(2 * j + core, TILE), :]


def gram_first_body(pos, tab, mine, r0, r1, r2, r3, across, down, right, turned, some, sems):
    copies = []
    for k, ref in enumerate((r0, r1, r2, r3)):
        lanes = tile_at(lax.bitwise_xor(pos[0], k))
        copies.append(
            pltpu.make_async_copy(ref.at[BLOCK : 2 * BLOCK, :], right.at[:, lanes], sems.at[k])
        )
        copies[k].start()
    turn(pos[1], mine, turned, some)
    across[...] = dot(some[...], turned[...])
    down[...] = dot(turned[...], mine[...]).astype(BF16)
    for copy in copies:
        copy.wait()


def gram_first(pos, tab, mine, sides):
    return call(
        gram_first_body,
        (),
        [whole()] + [outside()] * RING,
        [whole()] * 3,
        [
            jax.ShapeDtypeStruct((HALF, BLOCK), F32),
            jax.ShapeDtypeStruct((HALF, HALF), BF16),
            jax.ShapeDtypeStruct((BLOCK, HALF), BF16),
        ],
        scratch=[
            pltpu.VMEM((HALF, BLOCK), BF16),
            pltpu.VMEM((HALF, HALF), BF16),
            pltpu.SemaphoreType.DMA((RING,)),
        ],
        flops=2 * BLOCK * BLOCK * HALF,
        moved=4 * BLOCK * BLOCK,
    )(pos, tab, mine, *stay(sides))


def gram_body(
    pos, tab, mine, other, half, down, step, step_other, o0, o1, o2, o3, turned, some, across, down_other, held, sems
):
    core = pos[1]
    outs = (o0, o1, o2, o3)
    copies = []

    def send(k, n, low, high):
        copy = pltpu.make_async_copy(
            held.at[k, low:high, :], outs[k].at[low:high, :], sems.at[k, n]
        )
        copy.start()
        copies.append(copy)

    turn(core, other, turned, some)
    across[...] = (half[...] + dot(some[...], turned[...])).astype(BF16)
    for k in range(RING):
        plane = lax.bitwise_xor(pos[0], k)
        for t in range(BLOCK // TILE):
            at = slice(TILE * t, TILE * (t + 1))
            held[k, at, :] = across[rows_at(plane, TILE), at]
        send(k, 0, 0, BLOCK)
    down_other[...] = dot(turned[...], mine[...]).astype(BF16)
    for k in range(RING):
        plane = lax.bitwise_xor(pos[0], k)
        for j in range(RING):
            at = slice(TILE * j, TILE * (j + 1))
            lanes = tile_at(plane)
            held[k, rows_at(BLOCK // TILE + 2 * j + core, TILE), :] = down[at, lanes]
            held[k, rows_at(BLOCK // TILE + 2 * j + 1 - core, TILE), :] = down_other[at, lanes]
        held[k, 2 * BLOCK : 2 * BLOCK + 16, :] = step[...]
        held[k, 2 * BLOCK + 16 : SHARE, :] = step_other[...]
        send(k, 1, BLOCK, SHARE)
    for copy in copies:
        copy.wait()


def gram(pos, tab, mine, other, half, down, step, step_other):
    return call(
        gram_body,
        (),
        [whole()] * 6,
        [outside()] * RING,
        [pltpu.HBM((SHARE, TILE), BF16)] * RING,
        scratch=[
            pltpu.VMEM((HALF, BLOCK), BF16),
            pltpu.VMEM((HALF, HALF), BF16),
            pltpu.VMEM((HALF, BLOCK), BF16),
            pltpu.VMEM((HALF, HALF), BF16),
            pltpu.VMEM((RING, SHARE, TILE), BF16),
            pltpu.SemaphoreType.DMA((RING, 2)),
        ],
        flops=2 * BLOCK * BLOCK * HALF,
        moved=8 * BLOCK * HALF,
    )(pos, tab, mine, other, half, down, step, step_other)


def stats_body(
    pos, tab, left, right, g0, g1, g2, g3, new_left, new_right, vec, rows, cols, held, sems, gram_sems
):
    gets = [pltpu.make_async_copy(g, held.at[k], gram_sems.at[k]) for k, g in enumerate((g0, g1, g2, g3))]
    loads, stores = [], []
    for s in range(SLOTS):
        pairs = ((left, rows, new_left), (right, cols, new_right))
        loads += [
            pltpu.make_async_copy(a.at[s], b.at[s], sems.at[0, s, n])
            for n, (a, b, c) in enumerate(pairs)
        ]
        stores += [
            pltpu.make_async_copy(b.at[s], c.at[s], sems.at[1, s, n])
            for n, (a, b, c) in enumerate(pairs)
        ]
    for copy in gets + loads:
        copy.start()
    for k in range(RING):
        gets[k].wait()
        plane = lax.bitwise_xor(pos[0], k)
        vec[:, tile_at(2 * plane + pos[1])] = held[k, 2 * BLOCK : 2 * BLOCK + 16, :]
        vec[:, tile_at(2 * plane + 1 - pos[1])] = held[k, 2 * BLOCK + 16 : SHARE, :]
    for s in range(SLOTS):
        source = tab[T_REL + s]
        some = source >= 0
        k = jnp.maximum(source, 0)
        loads[2 * s].wait()
        for t in range(BLOCK // TILE):
            at = slice(TILE * t, TILE * (t + 1))
            add = jnp.where(some, held[k, at, :].astype(F32), 0.0)
            rows[s, :, at] = BETA_STAT * rows[s, :, at] + (1.0 - BETA_STAT) * add
        stores[2 * s].start()
        loads[2 * s + 1].wait()
        add = jnp.where(some, held[k, BLOCK : 2 * BLOCK, :].astype(F32), 0.0)
        cols[s] = BETA_STAT * cols[s] + (1.0 - BETA_STAT) * add
        stores[2 * s + 1].start()
    for copy in stores:
        copy.wait()


def stats(pos, tab, left, right, grams):
    return call(
        stats_body,
        (),
        [outside()] * (2 + RING),
        [outside(), outside(), whole()],
        [
            jax.ShapeDtypeStruct((SLOTS, TILE, BLOCK), F32),
            jax.ShapeDtypeStruct((SLOTS, BLOCK, TILE), F32),
            jax.ShapeDtypeStruct((16, BLOCK), BF16),
        ],
        scratch=[
            pltpu.VMEM((SLOTS, TILE, BLOCK), F32),
            pltpu.VMEM((SLOTS, BLOCK, TILE), F32),
            pltpu.VMEM((RING, SHARE, TILE), BF16),
            pltpu.SemaphoreType.DMA((2, SLOTS, 2)),
            pltpu.SemaphoreType.DMA((RING,)),
        ],
        moved=16 * SLOTS * BLOCK * TILE + 16 * BLOCK * TILE,
    )(pos, tab, *stay([left, right, *grams]))


def back_body(pos, tab, got, out):
    for i in range(PER):
        at = rows_at(tab[T_OWNER + RING * i + pos[0]])
        out[ROWS * i : ROWS * (i + 1), :] = got[at, :]


def back(pos, tab, got):
    return call(
        back_body,
        (),
        [whole()],
        whole(),
        jax.ShapeDtypeStruct((BODY, HALF), BF16),
        moved=2 * (BLOCK + BODY) * HALF,
    )(pos, tab, got)


def place_body(parts, pos, tab, *refs):
    out, rows, sems = refs[-3:]
    core = pos[1]
    copies = []
    for n, (k, first, count) in enumerate(parts):
        plane = lax.bitwise_xor(pos[0], k)
        ours, theirs = refs[2 * n], refs[2 * n + 1]
        for i in range(count):
            at = slice(ROWS * i, ROWS * (i + 1))
            slab = len(copies)
            here = slice(ROWS * slab, ROWS * (slab + 1))
            for j in range(RING):
                lanes = slice(TILE * j, TILE * (j + 1))
                rows[here, tile_at(2 * j + core)] = ours[at, lanes]
                rows[here, tile_at(2 * j + 1 - core)] = theirs[at, lanes]
            target = out.at[rows_at(tab[RING * (first + i) + plane]), :]
            copies.append(pltpu.make_async_copy(rows.at[here, :], target, sems.at[slab]))
            copies[-1].start()
    for copy in copies:
        copy.wait()


def place(pos, tab, parts, arrays, onto=None):
    def place_part(*refs):
        place_body(parts, *refs)

    slabs = sum(count for _, _, count in parts)
    extra = () if onto is None else (onto,)
    return pl.pallas_call(
        place_part,
        name="place_part",
        grid_spec=pltpu.PrefetchScalarGridSpec(
            num_scalar_prefetch=2,
            grid=(),
            in_specs=[whole()] * (2 * len(parts)) + [outside()] * len(extra),
            out_specs=outside(),
            scratch_shapes=[
                pltpu.VMEM((ROWS * slabs, BLOCK), BF16),
                pltpu.SemaphoreType.DMA((slabs,)),
            ],
        ),
        out_shape=jax.ShapeDtypeStruct((FULL, BLOCK), BF16),
        input_output_aliases={} if onto is None else {2 + 2 * len(parts): 0},
        compiler_params=pltpu.CompilerParams(vmem_limit_bytes=VMEM_LIMIT),
        cost_estimate=pl.CostEstimate(
            flops=0, bytes_accessed=4 * ROWS * slabs * BLOCK, transcendentals=0
        ),
    )(pos, tab, *arrays, *extra)


def hop(x, k):
    return lax.ppermute(x, "y", [(i, i ^ k) for i in range(RING)])


def swap(x):
    return lax.ppermute(x, "core", [(0, 1), (1, 0)])


def route(x):
    x = x.reshape(OWNERS, ROWS, HALF)
    return lax.all_to_all(x, ("x", "z"), 0, 0).reshape(BLOCK, HALF)


def shards(
    grads,
    vec_grads,
    factor_left,
    factor_right,
    root_left,
    root_right,
    vec_param,
    vec_first,
    vec_second,
    bucket_block,
    block_slot,
    decay_mask,
):
    y, core = lax.axis_index("y"), lax.axis_index("core")
    owner = lax.axis_index(("x", "z"))
    pos = jnp.stack([y, core, owner]).astype(jnp.int32)
    grad = grads.reshape(FULL, BLOCK)
    got, got_vec = swap(grad), swap(vec_grads)
    tab, own, vec = front(pos, jnp.concatenate([bucket_block, block_slot]), grad, vec_grads)
    give_a, keep_a, give_b, keep_b = pair(pos, tab, own, got, vec, got_vec)
    got_a, got_b = hop(give_a, 1), hop(give_b, 3)
    last_a = hop(keep_a[A_ROWS:] + got_a[A_ROWS:], 3)
    last_b = hop(keep_b[BS_ROWS:] + got_b[BS_ROWS:], 1)
    parts = [keep_a, got_a, last_a, keep_b, got_b, last_b]
    sides = roots(pos, tab, root_left, root_right)
    parts, sides = lax.optimization_barrier((parts, sides))
    send, new_first, new_second, step = total(
        pos, tab, parts, vec_param, vec_first, vec_second, decay_mask
    )
    send, sides = lax.optimization_barrier((send, sides))
    near, other_near, far = hop(sides[1], 1), hop(sides[3], 3), hop(sides[2], 2)
    mine = route(send)
    step_other = swap(step)
    mine, near, other_near, far, step_other = lax.optimization_barrier(
        (mine, near, other_near, far, step_other)
    )
    sides = [sides[0], near, far, other_near]
    other = swap(mine)
    across, down, right = gram_first(pos, tab, mine, sides)
    other, sides, across, down, right = lax.optimization_barrier(
        (other, sides, across, down, right)
    )
    grams = gram(pos, tab, mine, other, across, down, step, step_other)
    others = [swap(x) for x in sides]
    others, grams = lax.optimization_barrier((others, grams))
    result = update(pos, tab, mine, other, right, sides, others)
    result, grams = lax.optimization_barrier((result, grams))
    near, other_near, far = hop(grams[1], 1), hop(grams[3], 3), hop(grams[2], 2)
    got = route(result)
    got, near, other_near, far = lax.optimization_barrier((got, near, other_near, far))
    grams = [grams[0], near, far, other_near]
    piece = back(pos, tab, got)
    near, near_other = hop(piece, 3), hop(piece, 1)
    new_left, new_right, vec_update = stats(pos, tab, factor_left, factor_right, grams)
    near, near_other, new_left, new_right, vec_update = lax.optimization_barrier(
        (near, near_other, new_left, new_right, vec_update[0:1])
    )
    far = [hop(near[:A_ROWS], 1), hop(near_other[A_ROWS:], 3)]
    both = []
    for x in (piece, near, near_other):
        both += [x, swap(x)]
    placed = place(pos, tab, ((0, 0, PER), (3, 0, PER), (1, 0, PER)), both)
    far, placed = lax.optimization_barrier((far, placed))
    both = [far[0], swap(far[0]), far[1], swap(far[1])]
    block_update = place(pos, tab, ((2, 0, HEAD), (2, HEAD, PER - HEAD)), both, placed)
    return (
        block_update.reshape(NBLK, ROWS, BLOCK),
        new_left,
        new_right,
        vec_update,
        new_first,
        new_second,
    )


def solution(mesh):
    fine = Mesh(mesh.devices.reshape(RING, CORES, 4, 8), ("y", "core", "x", "z"))
    dp, shard = ("y", "core"), ("x", "z")
    return jax.shard_map(
        shards,
        mesh=fine,
        in_specs=(
            P(dp, None, shard, None),
            P(dp, shard, None),
            P(shard, dp, None),
            P(shard, None, dp),
            P(shard, None, dp),
            P(shard, None, dp),
            P(shard, dp),
            P(shard, dp),
            P(shard, dp),
            P(),
            P(),
            P(shard, dp),
        ),
        out_specs=(
            P(None, shard, None),
            P(shard, dp, None),
            P(shard, None, dp),
            P(shard, None),
            P(shard, dp),
            P(shard, dp),
        ),
        check_vma=False,
    )
```
